32 devices in a mesh: parts: 2 (over y), blk: 4 (over z), win: 2 (over x), frq: 2 (over core).
Axes of the slice: x: 2, y: 2, z: 4, core: 2. Of those that a mesh axis runs over, the one named last changes fastest.
Arguments:
- traces: bfloat16 [2048, 4, 2048], P(('parts', 'blk'), 'win'), parts along dimension 0, may hold values from -48 to 48
- block_members: int32 [32, 64], P(('parts', 'blk')), parts along dimension 0, may hold values from 0 to 1023, as said below
- pair_blocks: int32 [16, 2], P('parts'), parts along dimension 0, may hold values from 0 to 15, as said below
- pair_owner: int32 [16, 1], P('parts'), parts along dimension 0, may hold values from 0 to 3, as said below
Outputs:
- coherency: bfloat16 [2, 32, 64, 64, 512], P(None, ('parts', 'blk'), 'win', None, 'frq'), parts along dimension 1
The draws below stay inside these ranges and needn't reach their ends.
There are 2 independent parts, one for each index of `parts`. The reference program is written for one: setup_inputs(seed, part) draws one part's arguments, and reference() takes and returns one part's arrays. A program takes and returns all parts, laid end to end along the dimension named above; each array names one. Nothing has to cross between parts.
Inputs may be any that keep to these rules, and one draw needn't show every extreme that they name: `block_members`: row b holds the 64 stations of block b, all among the stations b // 4 * 4 * 64 to b // 4 * 4 * 64 + 4 * 64 - 1; every station lies in exactly one block. `pair_blocks`: row p is a pair (a, b) with a // 4 == p // 2 and a <= b <= a + 3; no pair appears twice; in each aligned group of 2 rows but the last, some pair has b among the next group's blocks. `pair_owner`: within each aligned group of 2 rows no owner is named twice; no owner is named more than 4 times in all, and some owner exactly 4 times; every owner is named.
All inputs are finite; a program needn't handle non-finite values.
Results may differ from the reference program's by a relative error of at most 0.0077.
Values may be sent and summed in bfloat16 or wider, within the bound.
A program may use at most 128 MiB of HBM per device.

```python
import math
import jax
import jax.numpy as jnp
from jax import lax

SEGMENT_LENGTH = 2048
FREQS = 512
BS = 64
REACH = 3
PAIR_DEV = 2
SB = 4
BLOCKS = 16
STATIONS = 1024
SEGMENT_TOTAL = 4
PAIRS = 8
OWNERS = 4
CAP = 4
N_WIN = 2


def draw_traces(key, part):
    key = jax.random.fold_in(key, 11)
    derived_seed_keys = jax.random.split(key, 8)
    noise_part = jax.random.normal(derived_seed_keys[0], (STATIONS, SEGMENT_TOTAL, SEGMENT_LENGTH), jnp.float32)
    shift_size = 1.5
    seismic_shock_share = 0.2
    gain_values = jnp.exp(jax.random.uniform(derived_seed_keys[1], (STATIONS, SEGMENT_TOTAL, 1), jnp.float32, -1.2, 1.2))
    offsets = jax.random.uniform(derived_seed_keys[2], (STATIONS, SEGMENT_TOTAL, 1), jnp.float32, -1.0, 1.0) * shift_size
    common = jax.random.normal(derived_seed_keys[3], (1, SEGMENT_TOTAL, SEGMENT_LENGTH), jnp.float32)
    coherence = jax.random.uniform(derived_seed_keys[4], (1, SEGMENT_TOTAL, 1), jnp.float32, 0.4, 1.2)
    transient_pulses = jnp.where(jax.random.uniform(derived_seed_keys[5], (1, SEGMENT_TOTAL, 1), jnp.float32) < seismic_shock_share, 6.0, 0.0)
    sinusoid_frequencies = jax.random.uniform(derived_seed_keys[6], (1, SEGMENT_TOTAL, 1), jnp.float32, 1.0, FREQS * 1.0)
    starting_angle_shifts = jax.random.uniform(derived_seed_keys[7], (1, SEGMENT_TOTAL, 1), jnp.float32, -3.14159, 3.14159)
    timing_points = jnp.arange(SEGMENT_LENGTH, dtype=jnp.float32).reshape(1, 1, SEGMENT_LENGTH)
    seismic_shocks = transient_pulses * jnp.cos(sinusoid_frequencies * timing_points * (6.283185307 / SEGMENT_LENGTH) + starting_angle_shifts)
    traces_out = offsets + gain_values * (noise_part + coherence * common + seismic_shocks)
    return jnp.clip(traces_out, -48.0, 48.0).astype(jnp.bfloat16)


def draw_block_members(key, part):
    key = jax.random.fold_in(key, 23)
    held_rows = SB * BS
    groups = BLOCKS // SB
    derived_seed_keys = jax.random.split(key, groups)

    def shuffled(one_key):
        return jax.random.permutation(one_key, held_rows)
    orders = jax.vmap(shuffled)(derived_seed_keys).astype(jnp.int32)
    offsets_row = (jnp.arange(groups, dtype=jnp.int32) * held_rows).reshape(groups, 1)
    return (orders + offsets_row).reshape(BLOCKS, BS).astype(jnp.int32)


def draw_pair_blocks(key, part):
    key = jax.random.fold_in(key, 37)
    groups = BLOCKS // SB
    span_size = REACH + 1
    cand_count = SB * span_size
    candidate = jnp.arange(cand_count, dtype=jnp.int32).reshape(1, cand_count)
    local_first = candidate // span_size
    distance = candidate % span_size
    group_ids = jnp.arange(groups, dtype=jnp.int32).reshape(groups, 1)
    first_block = group_ids * SB + local_first
    second_block = first_block + distance
    usable = second_block < BLOCKS
    crossing = (local_first == SB - 1) & (distance == 1) & usable
    scores = jax.random.randint(key, (groups, cand_count), 0, 1 << 16, dtype=jnp.int32)
    scores = scores * cand_count + candidate + 1
    scores = jnp.where(crossing, 1 << 30, scores)
    scores = jnp.where(usable, scores, -1 - candidate)
    chosen = jnp.sort(lax.top_k(scores, PAIR_DEV)[1], axis=1)
    first_pick = jnp.take_along_axis(jnp.broadcast_to(first_block, (groups, cand_count)), chosen, axis=1)
    second_pick = jnp.take_along_axis(second_block, chosen, axis=1)
    return jnp.stack([first_pick, second_pick], axis=-1).reshape(groups * PAIR_DEV, 2).astype(jnp.int32)


def draw_pair_owner(key, part):
    key = jax.random.fold_in(key, 53)
    order = jax.random.permutation(key, OWNERS).astype(jnp.int32)
    ranks = jnp.arange(OWNERS, dtype=jnp.int32)
    hot_count = OWNERS // 4
    loads = jnp.where(ranks < hot_count, CAP, jnp.where(ranks < 3 * hot_count, 1, PAIR_DEV)).astype(jnp.int32)
    run_ends = jnp.cumsum(loads).astype(jnp.int32)
    rows = jnp.arange(PAIRS, dtype=jnp.int32)
    position = rows % PAIR_DEV * OWNERS + rows // PAIR_DEV
    run_index = jnp.sum((position[:, None] >= run_ends[None, :]).astype(jnp.int32), axis=1)
    return jnp.take(order, run_index).reshape(PAIRS, 1).astype(jnp.int32)


def setup_inputs(seed: int = 0, part: int = 0) -> dict:
    keys = jax.random.split(jax.random.key(seed), 5)
    part_splits = jax.random.split(jax.random.fold_in(keys[4], part), 5)
    traces = draw_traces(jax.random.fold_in(jax.random.fold_in(keys[4], part), 71), part)
    block_members = draw_block_members(jax.random.fold_in(jax.random.fold_in(keys[4], part), 71), part)
    pair_blocks = draw_pair_blocks(jax.random.fold_in(jax.random.fold_in(keys[4], part), 71), part)
    pair_owner = draw_pair_owner(jax.random.fold_in(jax.random.fold_in(keys[4], part), 71), part)
    return {"traces": traces, "block_members": block_members, "pair_blocks": pair_blocks, "pair_owner": pair_owner}


eps_time = 1e-05
eps_power = 1e-06

def dft_table():
    sample_index = jnp.arange(SEGMENT_LENGTH, dtype=jnp.int32).reshape(SEGMENT_LENGTH, 1)
    bin_index = jnp.arange(FREQS, dtype=jnp.int32).reshape(1, FREQS) + 1
    angles = (sample_index * bin_index % SEGMENT_LENGTH).astype(jnp.float32) * (2.0 * math.pi / SEGMENT_LENGTH)
    return jnp.concatenate([jnp.cos(angles), jnp.sin(angles)], axis=1).astype(jnp.bfloat16)

def whiten_block(block_traces, table_values):
    values = block_traces.astype(jnp.float32)
    centre = values - lax.optimization_barrier(jnp.mean(values, axis=2, keepdims=True))
    spread = lax.optimization_barrier(jnp.mean(centre * centre, axis=2, keepdims=True))
    normal = (centre * lax.rsqrt(spread + eps_time)).astype(jnp.bfloat16)
    product = jnp.dot(normal.reshape(BS * SEGMENT_TOTAL, SEGMENT_LENGTH), table_values, preferred_element_type=jnp.float32)
    real_part = product[:, :FREQS].reshape(BS, SEGMENT_TOTAL, FREQS)
    imag_part = -product[:, FREQS:].reshape(BS, SEGMENT_TOTAL, FREQS)
    band_power = lax.optimization_barrier(jnp.sum(real_part * real_part + imag_part * imag_part, axis=1, keepdims=True)) / SEGMENT_TOTAL
    gain_factor = lax.rsqrt(band_power + eps_power)
    return jnp.stack([real_part * gain_factor, imag_part * gain_factor]).astype(jnp.bfloat16)

def pair_tile(first_block, second_block):
    group_windows = SEGMENT_TOTAL // N_WIN
    left_part = first_block.astype(jnp.float32).reshape(2, BS, N_WIN, group_windows, FREQS)
    right_part = second_block.astype(jnp.float32).reshape(2, BS, N_WIN, group_windows, FREQS)
    form = 'igwf,jgwf->gijf'
    real_sum = jnp.einsum(form, left_part[0], right_part[0]) + jnp.einsum(form, left_part[1], right_part[1])
    imag_sum = jnp.einsum(form, left_part[1], right_part[0]) - jnp.einsum(form, left_part[0], right_part[1])
    group_part = (jnp.stack([real_sum, imag_sum]) * (1.0 / SEGMENT_TOTAL)).astype(jnp.bfloat16)
    group_part = lax.optimization_barrier(group_part)
    return lax.optimization_barrier(jnp.sum(group_part.astype(jnp.float32), axis=1)).astype(jnp.bfloat16)

def reference(traces, block_members, pair_blocks, pair_owner):
    table_values = dft_table()

    def one_block(members):
        return whiten_block(jnp.take(traces, members, axis=0), table_values)
    whitened = lax.map(one_block, block_members)

    def one_pair(pair_row):
        first_block = lax.dynamic_index_in_dim(whitened, pair_row[0], 0, keepdims=False)
        second_block = lax.dynamic_index_in_dim(whitened, pair_row[1], 0, keepdims=False)
        return pair_tile(first_block, second_block)
    tile_values = lax.map(one_pair, pair_blocks)
    owner_ids = pair_owner[:, 0]
    pair_ids = jnp.arange(PAIRS, dtype=jnp.int32)
    earlier = (owner_ids[:, None] == owner_ids[None, :]) & (pair_ids[None, :] < pair_ids[:, None])
    rank_ids = lax.optimization_barrier(jnp.sum(earlier.astype(jnp.int32), axis=1))
    slot_ids = owner_ids * CAP + rank_ids
    stacked = jnp.zeros((2, OWNERS * CAP, BS, BS, FREQS), jnp.bfloat16)
    return stacked.at[:, slot_ids].set(jnp.moveaxis(tile_values, 1, 0))
```

```python
import functools
import math

import jax
import jax.numpy as jnp
import numpy as np
from jax import lax
from jax.experimental import pallas as pl
from jax.experimental.pallas import tpu as pltpu
from jax.sharding import PartitionSpec as P

FREQS = 512
PAIR_DEV = 2

eps_time = 1e-05
eps_power = 1e-06
MIB = 1024 * 1024


def dft_tables(samples, parts):
    bins_dev = FREQS // parts
    t = np.arange(samples, dtype=np.int64)[:, None]
    k = np.arange(1, FREQS + 1, dtype=np.int64)[None, :]
    angles = (t * k % samples).astype(np.float32) * np.float32(2.0 * math.pi / samples)
    cos = np.cos(angles.astype(np.float64)).reshape(samples, parts, bins_dev)
    sin = np.sin(angles.astype(np.float64)).reshape(samples, parts, bins_dev)
    table = np.concatenate([cos, -sin], axis=2).transpose(1, 0, 2)
    return table.astype(np.float32).astype(jnp.bfloat16)


def spectra_kernel(frq_ref, src_ref, x_ref, table_ref, *rest, row_tile, groups, width, win_dev):
    outs, spectra = rest[:-1], rest[-1]
    step = pl.program_id(0)
    bins = table_ref.shape[2] // 2
    x = x_ref[...].astype(jnp.float32)
    centre = x - jnp.mean(x, axis=1, keepdims=True)
    spread = jnp.mean(centre * centre, axis=1, keepdims=True)
    normal = (centre * lax.rsqrt(spread + eps_time)).astype(jnp.bfloat16)
    product = jnp.dot(normal, table_ref[0], preferred_element_type=jnp.float32)
    spectra[pl.ds(pl.multiple_of(step * row_tile, row_tile), row_tile), :] = product.astype(jnp.bfloat16)

    @pl.when(step == pl.num_programs(0) - 1)
    def _():
        rows = spectra.shape[0]
        chunk = win_dev * width
        base = 0
        for out, count in zip(outs, groups):

            def pick(n, carry, out=out, base=base):
                start = pl.multiple_of((base + n) * chunk, chunk)
                column = src_ref[pl.ds(start, chunk), :]
                lane = lax.broadcasted_iota(jnp.int32, (chunk, rows), 1)
                onehot = jnp.where(lane == column, 1.0, 0.0).astype(jnp.bfloat16)
                got = jnp.dot(onehot, spectra[...], preferred_element_type=jnp.float32)
                got = got.astype(jnp.bfloat16)
                out[n, 0:chunk, :] = got[:, :bins]
                out[n, chunk : 2 * chunk, :] = got[:, bins:]
                return carry

            lax.fori_loop(0, count, pick, 0)
            base += count


def spectra(frq, src, x, table, groups, width, win_dev):
    rows, samples = x.shape
    cols = table.shape[2]
    chunk = win_dev * width
    row_tile = rows // 2
    shapes = [jax.ShapeDtypeStruct((n, 2 * chunk, cols // 2), jnp.bfloat16) for n in groups]
    return pl.pallas_call(
        functools.partial(
            spectra_kernel, row_tile=row_tile, groups=groups, width=width, win_dev=win_dev
        ),
        grid_spec=pltpu.PrefetchScalarGridSpec(
            num_scalar_prefetch=1,
            grid=(rows // row_tile,),
            in_specs=[
                pl.BlockSpec(src.shape, lambda i, f: (0, 0)),
                pl.BlockSpec((row_tile, samples), lambda i, f: (i, 0)),
                pl.BlockSpec((1, samples, cols), lambda i, f: (f[0], 0, 0)),
            ],
            out_specs=[pl.BlockSpec(s.shape, lambda i, f: (0, 0, 0)) for s in shapes],
            scratch_shapes=[pltpu.VMEM((rows, cols), jnp.bfloat16)],
        ),
        out_shape=shapes,
        compiler_params=pltpu.CompilerParams(vmem_limit_bytes=48 * MIB),
        cost_estimate=pl.CostEstimate(
            flops=2 * rows * samples * cols, bytes_accessed=8 * MIB, transcendentals=rows
        ),
    )(frq, src, x, table)


def tiles_kernel(pick_ref, *refs, nwin, win_dev, first_rows, width):
    firsts, seconds = refs[:nwin], refs[nwin : 2 * nwin]
    out_ref, left, right = refs[2 * nwin :]
    slots = pl.num_programs(0)
    slot = pl.program_id(0)
    windows = nwin * win_dev
    bins = out_ref.shape[4]
    filled = pick_ref[slots + slot]

    @pl.when(filled == 0)
    def _():
        out_ref[...] = jnp.zeros_like(out_ref)

    @pl.when(filled != 0)
    def _():
        def whitened(ends, rows, scale):
            real, imag = [], []
            for ref in ends:
                view = ref[...].reshape(2, win_dev, rows, bins).astype(jnp.float32)
                for w in range(win_dev):
                    real.append(view[0, w])
                    imag.append(view[1, w])
            power = sum(r * r + i * i for r, i in zip(real, imag)) * (1.0 / windows)
            gain = lax.rsqrt(power + eps_power) * scale
            return [r * gain for r in real], [i * gain for i in imag]

        real, imag = whitened(firsts, first_rows, 1.0 / windows)
        for w in range(windows):
            for term, value in enumerate((real[w] + imag[w], real[w], imag[w])):
                for part in range(bins // 128):
                    left[part, term * windows + w] = value[:, part * 128 : part * 128 + 128]
        real, imag = whitened(seconds, width, 1.0)
        for w in range(windows):
            right[w] = real[w]
            right[windows + w] = real[w] + imag[w]
            right[2 * windows + w] = real[w] - imag[w]

        tile = 16
        for lane in range(0, bins, 128):

            def columns(t, carry, lane=lane):
                start = pl.multiple_of(t * tile, tile)
                held = [
                    right[n, pl.ds(start, tile), lane : lane + 128] for n in range(3 * windows)
                ]

                def row(i, c):
                    total = []
                    for term in range(3):
                        acc = None
                        for w in range(windows):
                            n = term * windows + w
                            one = left[lane // 128, n, pl.ds(i, 1), :]
                            prod = jnp.broadcast_to(one, (tile, 128)) * held[n]
                            acc = prod if acc is None else acc + prod
                        total.append(acc)
                    out_ref[0, 0, i, pl.ds(start, tile), lane : lane + 128] = (
                        total[0] - total[2]
                    ).astype(jnp.bfloat16)
                    out_ref[1, 0, i, pl.ds(start, tile), lane : lane + 128] = (
                        total[0] - total[1]
                    ).astype(jnp.bfloat16)
                    return c

                lax.fori_loop(0, first_rows, row, 0, unroll=8)
                return carry

            lax.fori_loop(0, width // tile, columns, 0)


def tiles(pick, firsts, seconds, slots, win_dev, width):
    nwin = len(firsts)
    bins = seconds[0].shape[2]
    first_rows = firsts[0].shape[1] // (2 * win_dev)
    shape = (2, slots, first_rows, width, bins)
    first_spec = pl.BlockSpec((1, 2 * win_dev * first_rows, bins), lambda s, p: (p[s], 0, 0))
    second_spec = pl.BlockSpec((1, 2 * win_dev * width, bins), lambda s, p: (p[s], 0, 0))
    windows = nwin * win_dev
    return pl.pallas_call(
        functools.partial(
            tiles_kernel, nwin=nwin, win_dev=win_dev, first_rows=first_rows, width=width
        ),
        grid_spec=pltpu.PrefetchScalarGridSpec(
            num_scalar_prefetch=1,
            grid=(slots,),
            in_specs=[first_spec] * nwin + [second_spec] * nwin,
            out_specs=pl.BlockSpec(
                (2, 1, first_rows, width, bins), lambda s, p: (0, s, 0, 0, 0)
            ),
            scratch_shapes=[
                pltpu.VMEM((bins // 128, 3 * windows, first_rows, 128), jnp.float32),
                pltpu.VMEM((3 * windows, width, bins), jnp.float32),
            ],
        ),
        out_shape=jax.ShapeDtypeStruct(shape, jnp.bfloat16),
        compiler_params=pltpu.CompilerParams(vmem_limit_bytes=48 * MIB),
        cost_estimate=pl.CostEstimate(
            flops=16 * windows * math.prod(shape), bytes_accessed=12 * MIB, transcendentals=0
        ),
    )(pick, *firsts, *seconds)


def shards(table, traces, block_members, pair_blocks, pair_owner):
    block_count, width = block_members.shape
    local_rows, win_dev, samples = traces.shape
    owners = lax.axis_size("blk")
    nwin = lax.axis_size("win")
    me = lax.axis_index("blk")
    my_win = lax.axis_index("win")
    frq = lax.axis_index("frq")
    pairs_dev = PAIR_DEV
    slots = 2 * pairs_dev
    half = width // nwin
    chunk = win_dev * width

    owner_groups = pair_owner[:, 0].reshape(owners, pairs_dev)
    ends = pair_blocks.reshape(owners, pairs_dev, 2)
    owner_list = jnp.arange(owners, dtype=jnp.int32)

    mine = lax.dynamic_index_in_dim(owner_groups, me, 0, keepdims=False)
    my_ends = lax.dynamic_index_in_dim(ends, me, 0, keepdims=False) - me * block_count
    hit_out = mine.reshape(1, -1) == owner_list.reshape(-1, 1)
    sent = jnp.any(hit_out, axis=1)
    picked = jnp.sum(
        hit_out[:, :, None] * my_ends[None, :, :], axis=1
    )
    first_block = jnp.where(sent, picked[:, 0], -1)
    second_block = jnp.where(sent & (picked[:, 1] < block_count), picked[:, 1], -1)
    before = lax.dynamic_index_in_dim(ends, jnp.maximum(me - 1, 0), 0, keepdims=False)
    spill_block = before[:, 1] - me * block_count
    spill_block = jnp.where((spill_block >= 0) & (spill_block < block_count), spill_block, -1)

    members = block_members % local_rows
    window = jnp.arange(win_dev, dtype=jnp.int32)
    rows_block = (members[:, None, :] * win_dev + window.reshape(1, -1, 1)).reshape(
        block_count, chunk
    )

    def chosen(blocks, rows):
        onehot = blocks.reshape(-1, 1) == jnp.arange(block_count, dtype=jnp.int32).reshape(1, -1)
        value = jnp.sum(onehot[:, :, None] * rows[None], axis=1)
        return jnp.where(blocks.reshape(-1, 1) >= 0, value, -1)

    src = jnp.concatenate(
        [
            chosen(spill_block, rows_block),
            chosen(first_block, rows_block),
            chosen(second_block, rows_block),
        ]
    ).reshape(-1, 1)
    spill, first_send, second_local = spectra(
        frq.reshape(1).astype(jnp.int32),
        src,
        traces.reshape(local_rows * win_dev, samples),
        table,
        (pairs_dev, owners, owners),
        width,
        win_dev,
    )

    spilled = lax.ppermute(spill, "blk", [(n, n - 1) for n in range(1, owners)])
    first_in = lax.all_to_all(first_send, "blk", split_axis=0, concat_axis=0, tiled=True)
    from_next = hit_out & (my_ends[:, 1] >= block_count)[None, :]
    second_send = second_local
    for q in range(pairs_dev):
        second_send = jnp.where(from_next[:, q].reshape(-1, 1, 1), spilled[q][None], second_send)
    second_in = lax.all_to_all(second_send, "blk", split_axis=0, concat_axis=0, tiled=True)

    bins = first_in.shape[2]
    split = first_in.reshape(owners, 2 * win_dev, nwin, half, bins)

    def part(index):
        return lax.dynamic_index_in_dim(split, index, 2, keepdims=False).reshape(
            owners, 2 * win_dev * half, bins
        )

    firsts, seconds = [part(my_win)], [second_in]
    for shift in range(1, nwin):
        order = [(n, (n + shift) % nwin) for n in range(nwin)]
        firsts.append(lax.ppermute(part((my_win + shift) % nwin), "win", order))
        seconds.append(lax.ppermute(second_in, "win", order))

    hit_in = jnp.any(owner_groups == me, axis=1).astype(jnp.int32)
    rank = jnp.cumsum(hit_in) - hit_in
    of_slot = (hit_in.reshape(1, -1) == 1) & (
        rank.reshape(1, -1) == jnp.arange(slots, dtype=jnp.int32).reshape(-1, 1)
    )
    source = jnp.sum(of_slot * owner_list.reshape(1, -1), axis=1)
    filled = jnp.any(of_slot, axis=1).astype(jnp.int32)
    pick = jnp.concatenate([source, filled]).astype(jnp.int32)
    return tiles(pick, firsts, seconds, slots, win_dev, width)


def solution(mesh):
    placed = (
        P(("parts", "blk"), "win", None),
        P(("parts", "blk"), None),
        P("parts", None),
        P("parts", None),
    )

    def whole(traces, block_members, pair_blocks, pair_owner):
        table = jnp.asarray(dft_tables(traces.shape[2], mesh.shape["frq"]))
        return jax.shard_map(
            shards,
            mesh=mesh,
            in_specs=(P(None, None, None),) + placed,
            out_specs=P(None, ("parts", "blk"), "win", None, "frq"),
            check_vma=False,
        )(table, traces, block_members, pair_blocks, pair_owner)

    return whole
```

```python
import functools
import math

import jax
import jax.numpy as jnp
import numpy as np
from jax import lax
from jax.experimental import pallas as pl
from jax.experimental.pallas import tpu as pltpu
from jax.sharding import PartitionSpec as P

FREQS = 512
PAIR_DEV = 2

eps_time = 1e-05
eps_power = 1e-06
MIB = 1024 * 1024


def dft_tables(samples, parts):
    bins_dev = FREQS // parts
    t = np.arange(samples, dtype=np.int64)[:, None]
    k = np.arange(1, FREQS + 1, dtype=np.int64)[None, :]
    angles = (t * k % samples).astype(np.float32) * np.float32(2.0 * math.pi / samples)
    cos = np.cos(angles.astype(np.float64)).reshape(samples, parts, bins_dev)
    sin = np.sin(angles.astype(np.float64)).reshape(samples, parts, bins_dev)
    table = np.concatenate([cos, -sin], axis=2).transpose(1, 0, 2)
    return table.astype(np.float32).astype(jnp.bfloat16)


def spectra_kernel(
    meta_ref, blocks_ref, owner_ref, members_ref, x_ref, table_ref,
    spill, first_send, second_local, mask, pick, spectra, perm, *, row_tile, win_dev,
):
    step = pl.program_id(0)
    block_count, width = members_ref.shape
    owners, nwin, first_rows, bins = first_send.shape
    pairs_dev = spill.shape[0]
    slots = pick.shape[0] // 2
    x = x_ref[...].astype(jnp.float32)
    centre = x - jnp.mean(x, axis=1, keepdims=True)
    spread = jnp.mean(centre * centre, axis=1, keepdims=True)
    normal = (centre * lax.rsqrt(spread + eps_time)).astype(jnp.bfloat16)
    product = jnp.dot(normal, table_ref[0], preferred_element_type=jnp.float32)
    start = pl.multiple_of(step * row_tile, row_tile)
    spectra[pl.ds(start, row_tile), :] = product.astype(jnp.bfloat16)

    @pl.when(step == pl.num_programs(0) - 1)
    def _():
        me = meta_ref[0]
        rows = spectra.shape[0]
        chunk = win_dev * width
        half = width // nwin
        local = members_ref[...] % (rows // win_dev) * win_dev
        place = jnp.concatenate([local + w for w in range(win_dev)], axis=1)
        for block in range(block_count):
            row = lax.broadcasted_iota(jnp.int32, (rows, chunk), 0)
            onehot = jnp.where(row == place[block : block + 1, :], 1.0, 0.0).astype(jnp.bfloat16)
            perm[block] = lax.dot_general(
                onehot, spectra[...], (((0,), (0,)), ((), ())), preferred_element_type=jnp.float32
            ).astype(jnp.bfloat16)

        def whole_block(out, n, block):
            inside = (block >= 0) & (block < block_count)

            @pl.when(inside)
            def _():
                for part in range(2):
                    out[n, part * chunk : part * chunk + chunk, :] = perm[
                        block, :, part * bins : part * bins + bins
                    ]

            @pl.when(jnp.logical_not(inside))
            def _():
                out[n] = jnp.zeros(out.shape[1:], out.dtype)

        def halves(n, block):
            @pl.when(block >= 0)
            def _():
                for h in range(nwin):
                    for part in range(2):
                        for w in range(win_dev):
                            at = (part * win_dev + w) * half
                            first_send[n, h, at : at + half, :] = perm[
                                block,
                                w * width + h * half : w * width + h * half + half,
                                part * bins : part * bins + bins,
                            ]

            @pl.when(block < 0)
            def _():
                first_send[n] = jnp.zeros(first_send.shape[1:], first_send.dtype)

        before = jnp.maximum(me - 1, 0) * pairs_dev
        for q in range(pairs_dev):
            whole_block(spill, q, blocks_ref[(before + q) * 2 + 1] - me * block_count)

        def to_owner(o, carry):
            first, second = jnp.int32(-1), jnp.int32(-1)
            for q in range(pairs_dev):
                pair = me * pairs_dev + q
                hit = owner_ref[pair] == o
                first_end = blocks_ref[2 * pair] - me * block_count
                second_end = blocks_ref[2 * pair + 1] - me * block_count
                first = jnp.where(hit, first_end, first)
                second = jnp.where(hit, second_end, second)
                value = jnp.where(hit & (second_end >= block_count), 1.0, 0.0)
                mask[o, q : q + 1, :] = jnp.full((1, bins), value, jnp.float32)
            halves(o, first)
            whole_block(second_local, o, second)
            return carry

        lax.fori_loop(0, owners, to_owner, 0)

        for n in range(2 * slots):
            pick[n] = 0

        def from_group(g, rank):
            hit = owner_ref[g * pairs_dev] == me
            for q in range(1, pairs_dev):
                hit = hit | (owner_ref[g * pairs_dev + q] == me)

            @pl.when(hit & (rank < slots))
            def _():
                pick[rank] = g
                pick[slots + rank] = 1

            return rank + hit.astype(jnp.int32)

        lax.fori_loop(0, owners, from_group, jnp.int32(0))


def spectra(meta, pair_blocks, pair_owner, members, x, table, owners, nwin, win_dev, slots):
    rows, samples = x.shape
    cols = table.shape[2]
    bins = cols // 2
    block_count, width = members.shape
    chunk = win_dev * width
    row_tile = rows // 2
    whole = 2 * chunk
    shapes = [
        jax.ShapeDtypeStruct((PAIR_DEV, whole, bins), jnp.bfloat16),
        jax.ShapeDtypeStruct((owners, nwin, whole // nwin, bins), jnp.bfloat16),
        jax.ShapeDtypeStruct((owners, whole, bins), jnp.bfloat16),
        jax.ShapeDtypeStruct((owners, PAIR_DEV, bins), jnp.float32),
        jax.ShapeDtypeStruct((2 * slots,), jnp.int32),
    ]

    def fixed(shape):
        return pl.BlockSpec(shape, lambda i, *_: (0,) * len(shape))

    return pl.pallas_call(
        functools.partial(spectra_kernel, row_tile=row_tile, win_dev=win_dev),
        grid_spec=pltpu.PrefetchScalarGridSpec(
            num_scalar_prefetch=3,
            grid=(rows // row_tile,),
            in_specs=[
                fixed(members.shape),
                pl.BlockSpec((row_tile, samples), lambda i, *_: (i, 0)),
                pl.BlockSpec((1, samples, cols), lambda i, m, *_: (m[1], 0, 0)),
            ],
            out_specs=[fixed(s.shape) for s in shapes[:-1]]
            + [pl.BlockSpec(memory_space=pltpu.SMEM)],
            scratch_shapes=[
                pltpu.VMEM((rows, cols), jnp.bfloat16),
                pltpu.VMEM((block_count, chunk, cols), jnp.bfloat16),
            ],
        ),
        out_shape=shapes,
        compiler_params=pltpu.CompilerParams(vmem_limit_bytes=48 * MIB),
        cost_estimate=pl.CostEstimate(
            flops=2 * rows * samples * cols, bytes_accessed=8 * MIB, transcendentals=rows
        ),
    )(meta, pair_blocks, pair_owner, members, x, table)


def exchange_kernel(
    n, nwin, spill, first_send, second_local, mask,
    first_out, second_out, first_x, second_x,
    spill_in, second_send,
    spill_sems, zf_send, zf_recv, zs_send, zs_recv, xf_send, xf_recv, xs_send, xs_recv, own_sems,
):
    me = lax.axis_index("blk")
    my_win = lax.axis_index("win")
    pairs_dev = spill.shape[0]

    def along(d):
        return {"blk": lax.rem(me + d, n)}

    def across(shift):
        return {"win": lax.rem(my_win + shift, nwin)}

    def remote(src, dst, send, recv, device):
        return pltpu.make_async_remote_copy(
            src_ref=src, dst_ref=dst, send_sem=send, recv_sem=recv,
            device_id=device, device_id_type=pl.DeviceIdType.MESH,
        )

    barrier = pltpu.get_barrier_semaphore()
    for d in range(1, n):
        pl.semaphore_signal(barrier, inc=1, device_id=along(d), device_id_type=pl.DeviceIdType.MESH)
    for s in range(1, nwin):
        pl.semaphore_signal(barrier, inc=1, device_id=across(s), device_id_type=pl.DeviceIdType.MESH)
    pl.semaphore_wait(barrier, n + nwin - 2)

    to_left = remote(spill, spill_in, spill_sems.at[0], spill_sems.at[1], along(n - 1))

    @pl.when(me > 0)
    def _():
        to_left.start()

    def first_to(d):
        return remote(
            first_send.at[lax.rem(me + d, n)], first_out.at[me], zf_send.at[d], zf_recv.at[d], along(d)
        )

    def second_to(d):
        return remote(
            second_send.at[lax.rem(me + d, n)], second_out.at[me], zs_send.at[d], zs_recv.at[d], along(d)
        )

    def first_across(d, shift):
        source = lax.rem(me + n - d, n)
        other = lax.rem(my_win + shift, nwin)
        ref = first_send if d == 0 else first_out
        k = d * nwin + shift
        return remote(
            ref.at[source, other], first_x.at[shift - 1, source], xf_send.at[k], xf_recv.at[k], across(shift)
        )

    def second_across(d, shift):
        source = lax.rem(me + n - d, n)
        ref = second_send if d == 0 else second_out
        k = d * nwin + shift
        return remote(
            ref.at[source], second_x.at[shift - 1, source], xs_send.at[k], xs_recv.at[k], across(shift)
        )

    order = sorted(range(1, n), key=lambda d: min(d, n - d))
    for d in order:
        first_to(d).start()
    own_first = pltpu.make_async_copy(first_send.at[me], first_out.at[me], own_sems.at[0])
    own_first.start()
    for shift in range(1, nwin):
        first_across(0, shift).start()

    @pl.when(me == n - 1)
    def _():
        spill_in[...] = jnp.zeros_like(spill_in)

    @pl.when(me < n - 1)
    def _():
        to_left.wait_recv()

    for d in order + [0]:
        o = lax.rem(me + d, n)
        total = second_local[o].astype(jnp.float32)
        for q in range(pairs_dev):
            total = total + spill_in[q].astype(jnp.float32) * mask[o, q : q + 1, :]
        second_send[o] = total.astype(jnp.bfloat16)
        if d:
            second_to(d).start()
    own_second = pltpu.make_async_copy(second_send.at[me], second_out.at[me], own_sems.at[1])
    own_second.start()
    for shift in range(1, nwin):
        second_across(0, shift).start()

    for d in order:
        first_to(d).wait_recv()
        for shift in range(1, nwin):
            first_across(d, shift).start()
    for d in order:
        second_to(d).wait_recv()
        for shift in range(1, nwin):
            second_across(d, shift).start()
    own_first.wait()
    own_second.wait()

    @pl.when(me > 0)
    def _():
        to_left.wait_send()

    for d in order:
        first_to(d).wait_send()
        second_to(d).wait_send()
    for d in range(n):
        for shift in range(1, nwin):
            first_across(d, shift).wait()
            second_across(d, shift).wait()


def exchange(spill, first_send, second_local, mask):
    n, nwin, first_rows, bins = first_send.shape
    rows = second_local.shape[1]
    hbm = pl.BlockSpec(memory_space=pl.ANY)
    vmem = pl.BlockSpec(memory_space=pltpu.VMEM)
    dma = pltpu.SemaphoreType.DMA
    sent = jax.ShapeDtypeStruct
    return pl.pallas_call(
        functools.partial(exchange_kernel, n, nwin),
        in_specs=[hbm, hbm, vmem, vmem],
        out_specs=[hbm] * 4,
        out_shape=[
            sent(first_send.shape, jnp.bfloat16),
            sent(second_local.shape, jnp.bfloat16),
            sent((nwin - 1, n, first_rows, bins), jnp.bfloat16),
            sent((nwin - 1, n, rows, bins), jnp.bfloat16),
        ],
        scratch_shapes=[
            pltpu.VMEM(spill.shape, jnp.bfloat16),
            pltpu.VMEM(second_local.shape, jnp.bfloat16),
            dma((2,)),
            dma((n,)), dma((n,)), dma((n,)), dma((n,)),
            dma((n * nwin,)), dma((n * nwin,)), dma((n * nwin,)), dma((n * nwin,)),
            dma((2,)),
        ],
        compiler_params=pltpu.CompilerParams(
            collective_id=0, has_side_effects=True, vmem_limit_bytes=32 * MIB
        ),
        cost_estimate=pl.CostEstimate(flops=0, bytes_accessed=4 * MIB, transcendentals=0),
    )(spill, first_send, second_local, mask)


def tiles_kernel(meta_ref, pick_ref, *refs, nwin, win_dev, first_rows, width):
    firsts, seconds = refs[:nwin], refs[nwin : 2 * nwin]
    out_ref, left, right = refs[2 * nwin :]
    slots = pl.num_programs(0)
    slot = pl.program_id(0)
    windows = nwin * win_dev
    bins = out_ref.shape[4]
    filled = pick_ref[slots + slot]

    @pl.when(filled == 0)
    def _():
        out_ref[...] = jnp.zeros_like(out_ref)

    @pl.when(filled != 0)
    def _():
        def whitened(ends, rows, scale):
            real, imag = [], []
            for ref in ends:
                view = ref[...].reshape(2, win_dev, rows, bins).astype(jnp.float32)
                for w in range(win_dev):
                    real.append(view[0, w])
                    imag.append(view[1, w])
            power = sum(r * r + i * i for r, i in zip(real, imag)) * (1.0 / windows)
            gain = lax.rsqrt(power + eps_power) * scale
            return [r * gain for r in real], [i * gain for i in imag]

        real, imag = whitened(firsts, first_rows, 1.0 / windows)
        for w in range(windows):
            for term, value in enumerate((real[w] + imag[w], real[w], imag[w])):
                for part in range(bins // 128):
                    left[part, term * windows + w] = value[:, part * 128 : part * 128 + 128]
        real, imag = whitened(seconds, width, 1.0)
        for w in range(windows):
            right[w] = real[w]
            right[windows + w] = real[w] + imag[w]
            right[2 * windows + w] = real[w] - imag[w]

        tile = 16
        for lane in range(0, bins, 128):

            def columns(t, carry, lane=lane):
                start = pl.multiple_of(t * tile, tile)
                held = [
                    right[n, pl.ds(start, tile), lane : lane + 128] for n in range(3 * windows)
                ]

                def row(i, c):
                    total = []
                    for term in range(3):
                        acc = None
                        for w in range(windows):
                            n = term * windows + w
                            one = left[lane // 128, n, pl.ds(i, 1), :]
                            prod = jnp.broadcast_to(one, (tile, 128)) * held[n]
                            acc = prod if acc is None else acc + prod
                        total.append(acc)
                    out_ref[0, 0, i, pl.ds(start, tile), lane : lane + 128] = (
                        total[0] - total[2]
                    ).astype(jnp.bfloat16)
                    out_ref[1, 0, i, pl.ds(start, tile), lane : lane + 128] = (
                        total[0] - total[1]
                    ).astype(jnp.bfloat16)
                    return c

                lax.fori_loop(0, first_rows, row, 0, unroll=8)
                return carry

            lax.fori_loop(0, width // tile, columns, 0)


def tiles(meta, pick, first_in, second_in, first_x, second_x, slots, win_dev, width):
    nwin, first_in_rows, bins = first_in.shape[1:]
    first_rows = first_in_rows // (2 * win_dev)
    whole = second_in.shape[1]
    shape = (2, slots, first_rows, width, bins)
    first_specs = [
        pl.BlockSpec((1, 1, first_in_rows, bins), lambda s, m, p: (p[s], m[2], 0, 0))
    ] + [
        pl.BlockSpec((1, 1, first_in_rows, bins), lambda s, m, p, k=k: (k, p[s], 0, 0))
        for k in range(nwin - 1)
    ]
    second_specs = [pl.BlockSpec((1, whole, bins), lambda s, m, p: (p[s], 0, 0))] + [
        pl.BlockSpec((1, 1, whole, bins), lambda s, m, p, k=k: (k, p[s], 0, 0))
        for k in range(nwin - 1)
    ]
    windows = nwin * win_dev
    return pl.pallas_call(
        functools.partial(
            tiles_kernel, nwin=nwin, win_dev=win_dev, first_rows=first_rows, width=width
        ),
        grid_spec=pltpu.PrefetchScalarGridSpec(
            num_scalar_prefetch=2,
            grid=(slots,),
            in_specs=first_specs + second_specs,
            out_specs=pl.BlockSpec(
                (2, 1, first_rows, width, bins), lambda s, m, p: (0, s, 0, 0, 0)
            ),
            scratch_shapes=[
                pltpu.VMEM((bins // 128, 3 * windows, first_rows, 128), jnp.float32),
                pltpu.VMEM((3 * windows, width, bins), jnp.float32),
            ],
        ),
        out_shape=jax.ShapeDtypeStruct(shape, jnp.bfloat16),
        compiler_params=pltpu.CompilerParams(vmem_limit_bytes=48 * MIB),
        cost_estimate=pl.CostEstimate(
            flops=16 * windows * math.prod(shape), bytes_accessed=12 * MIB, transcendentals=0
        ),
    )(meta, pick, first_in, *[first_x] * (nwin - 1), second_in, *[second_x] * (nwin - 1))


def shards(table, traces, block_members, pair_blocks, pair_owner):
    width = block_members.shape[1]
    local_rows, win_dev, samples = traces.shape
    owners = lax.axis_size("blk")
    nwin = lax.axis_size("win")
    slots = 2 * PAIR_DEV
    meta = jnp.stack([lax.axis_index(name) for name in ("blk", "frq", "win")]).astype(jnp.int32)
    spill, first_send, second_local, mask, pick = spectra(
        meta,
        pair_blocks.reshape(-1),
        pair_owner.reshape(-1),
        block_members,
        traces.reshape(local_rows * win_dev, samples),
        table,
        owners,
        nwin,
        win_dev,
        slots,
    )
    arrived = exchange(spill, first_send, second_local, mask)
    return tiles(meta, pick, *arrived, slots, win_dev, width)


def solution(mesh):
    placed = (
        P(("parts", "blk"), "win", None),
        P(("parts", "blk"), None),
        P("parts", None),
        P("parts", None),
    )

    def whole(traces, block_members, pair_blocks, pair_owner):
        table = jnp.asarray(dft_tables(traces.shape[2], mesh.shape["frq"]))
        return jax.shard_map(
            shards,
            mesh=mesh,
            in_specs=(P(None, None, None),) + placed,
            out_specs=P(None, ("parts", "blk"), "win", None, "frq"),
            check_vma=False,
        )(table, traces, block_members, pair_blocks, pair_owner)

    return whole
```

```python
import functools
import math

import jax
import jax.numpy as jnp
import numpy as np
from jax import lax
from jax.experimental import pallas as pl
from jax.experimental.pallas import tpu as pltpu
from jax.sharding import PartitionSpec as P

FREQS = 512
PAIR_DEV = 2

eps_time = 1e-05
eps_power = 1e-06
MIB = 1024 * 1024


def dft_tables(samples, parts):
    bins_dev = FREQS // parts
    t = np.arange(samples, dtype=np.int64)[:, None]
    k = np.arange(1, FREQS + 1, dtype=np.int64)[None, :]
    angles = (t * k % samples).astype(np.float32) * np.float32(2.0 * math.pi / samples)
    cos = np.cos(angles.astype(np.float64)).reshape(samples, parts, bins_dev)
    sin = np.sin(angles.astype(np.float64)).reshape(samples, parts, bins_dev)
    table = np.concatenate([cos, -sin], axis=2).transpose(1, 0, 2)
    return table.astype(np.float32).astype(jnp.bfloat16)


def spectra_kernel(
    meta_ref, blocks_ref, owner_ref, members_ref, x_ref, table_ref,
    spill, first_send, second_local, mask, pick, spectra, perm, *, row_tile, win_dev,
):
    step = pl.program_id(0)
    block_count, width = members_ref.shape
    owners, nwin, first_rows, bins = first_send.shape
    pairs_dev = spill.shape[0]
    slots = pick.shape[0] // 2
    x = x_ref[...].astype(jnp.float32)
    centre = x - jnp.mean(x, axis=1, keepdims=True)
    spread = jnp.mean(centre * centre, axis=1, keepdims=True)
    normal = (centre * lax.rsqrt(spread + eps_time)).astype(jnp.bfloat16)
    product = jnp.dot(normal, table_ref[0], preferred_element_type=jnp.float32)
    start = pl.multiple_of(step * row_tile, row_tile)
    spectra[pl.ds(start, row_tile), :] = product.astype(jnp.bfloat16)

    @pl.when(step == pl.num_programs(0) - 1)
    def _():
        me = meta_ref[0]
        rows = spectra.shape[0]
        chunk = win_dev * width
        half = width // nwin
        local = members_ref[...] % (rows // win_dev) * win_dev
        place = jnp.concatenate([local + w for w in range(win_dev)], axis=1)
        for block in range(block_count):
            row = lax.broadcasted_iota(jnp.int32, (rows, chunk), 0)
            onehot = jnp.where(row == place[block : block + 1, :], 1.0, 0.0).astype(jnp.bfloat16)
            perm[block] = lax.dot_general(
                onehot, spectra[...], (((0,), (0,)), ((), ())), preferred_element_type=jnp.float32
            ).astype(jnp.bfloat16)

        def whole_block(out, n, block):
            inside = (block >= 0) & (block < block_count)

            @pl.when(inside)
            def _():
                for part in range(2):
                    out[n, part * chunk : part * chunk + chunk, :] = perm[
                        block, :, part * bins : part * bins + bins
                    ]

            @pl.when(jnp.logical_not(inside))
            def _():
                out[n] = jnp.zeros(out.shape[1:], out.dtype)

        def halves(n, block):
            @pl.when(block >= 0)
            def _():
                for h in range(nwin):
                    for part in range(2):
                        for w in range(win_dev):
                            at = (part * win_dev + w) * half
                            first_send[n, h, at : at + half, :] = perm[
                                block,
                                w * width + h * half : w * width + h * half + half,
                                part * bins : part * bins + bins,
                            ]

            @pl.when(block < 0)
            def _():
                first_send[n] = jnp.zeros(first_send.shape[1:], first_send.dtype)

        before = jnp.maximum(me - 1, 0) * pairs_dev
        for q in range(pairs_dev):
            whole_block(spill, q, blocks_ref[(before + q) * 2 + 1] - me * block_count)

        def to_owner(o, carry):
            first, second = jnp.int32(-1), jnp.int32(-1)
            for q in range(pairs_dev):
                pair = me * pairs_dev + q
                hit = owner_ref[pair] == o
                first_end = blocks_ref[2 * pair] - me * block_count
                second_end = blocks_ref[2 * pair + 1] - me * block_count
                first = jnp.where(hit, first_end, first)
                second = jnp.where(hit, second_end, second)
                value = jnp.where(hit & (second_end >= block_count), 1.0, 0.0)
                mask[o, q : q + 1, :] = jnp.full((1, bins), value, jnp.float32)
            halves(o, first)
            whole_block(second_local, o, second)
            return carry

        lax.fori_loop(0, owners, to_owner, 0)

        for n in range(2 * slots):
            pick[n] = 0

        def from_group(g, rank):
            hit = owner_ref[g * pairs_dev] == me
            for q in range(1, pairs_dev):
                hit = hit | (owner_ref[g * pairs_dev + q] == me)

            @pl.when(hit & (rank < slots))
            def _():
                pick[rank] = g
                pick[slots + rank] = 1

            return rank + hit.astype(jnp.int32)

        lax.fori_loop(0, owners, from_group, jnp.int32(0))


def spectra(meta, pair_blocks, pair_owner, members, x, table, owners, nwin, win_dev, slots):
    rows, samples = x.shape
    cols = table.shape[2]
    bins = cols // 2
    block_count, width = members.shape
    chunk = win_dev * width
    row_tile = rows // 2
    whole = 2 * chunk
    shapes = [
        jax.ShapeDtypeStruct((PAIR_DEV, whole, bins), jnp.bfloat16),
        jax.ShapeDtypeStruct((owners, nwin, whole // nwin, bins), jnp.bfloat16),
        jax.ShapeDtypeStruct((owners, whole, bins), jnp.bfloat16),
        jax.ShapeDtypeStruct((owners, PAIR_DEV, bins), jnp.float32),
        jax.ShapeDtypeStruct((2 * slots,), jnp.int32),
    ]

    def fixed(shape):
        return pl.BlockSpec(shape, lambda i, *_: (0,) * len(shape))

    return pl.pallas_call(
        functools.partial(spectra_kernel, row_tile=row_tile, win_dev=win_dev),
        grid_spec=pltpu.PrefetchScalarGridSpec(
            num_scalar_prefetch=3,
            grid=(rows // row_tile,),
            in_specs=[
                fixed(members.shape),
                pl.BlockSpec((row_tile, samples), lambda i, *_: (i, 0)),
                pl.BlockSpec((1, samples, cols), lambda i, m, *_: (m[1], 0, 0)),
            ],
            out_specs=[fixed(s.shape) for s in shapes[:-1]]
            + [pl.BlockSpec(memory_space=pltpu.SMEM)],
            scratch_shapes=[
                pltpu.VMEM((rows, cols), jnp.bfloat16),
                pltpu.VMEM((block_count, chunk, cols), jnp.bfloat16),
            ],
        ),
        out_shape=shapes,
        compiler_params=pltpu.CompilerParams(vmem_limit_bytes=48 * MIB),
        cost_estimate=pl.CostEstimate(
            flops=2 * rows * samples * cols, bytes_accessed=8 * MIB, transcendentals=rows
        ),
    )(meta, pair_blocks, pair_owner, members, x, table)


def exchange_kernel(
    n, nwin, spill, first_send, second_local, mask,
    first_out, second_out, first_x, second_x,
    spill_in, second_send,
    spill_sems, zf_send, zf_recv, zs_send, zs_recv, xf_send, xf_recv, xs_send, xs_recv, own_sems,
):
    me = lax.axis_index("blk")
    my_win = lax.axis_index("win")
    pairs_dev = spill.shape[0]

    def along(d):
        return {"blk": lax.rem(me + d, n)}

    def across(shift):
        return {"win": lax.rem(my_win + shift, nwin)}

    def remote(src, dst, send, recv, device):
        return pltpu.make_async_remote_copy(
            src_ref=src, dst_ref=dst, send_sem=send, recv_sem=recv,
            device_id=device, device_id_type=pl.DeviceIdType.MESH,
        )

    barrier = pltpu.get_barrier_semaphore()
    for d in range(1, n):
        pl.semaphore_signal(barrier, inc=1, device_id=along(d), device_id_type=pl.DeviceIdType.MESH)
    for s in range(1, nwin):
        pl.semaphore_signal(barrier, inc=1, device_id=across(s), device_id_type=pl.DeviceIdType.MESH)
    pl.semaphore_wait(barrier, n + nwin - 2)

    to_left = remote(spill, spill_in, spill_sems.at[0], spill_sems.at[1], along(n - 1))

    @pl.when(me > 0)
    def _():
        to_left.start()

    def first_to(d):
        return remote(
            first_send.at[lax.rem(me + d, n)], first_out.at[me], zf_send.at[d], zf_recv.at[d], along(d)
        )

    def second_to(d):
        return remote(
            second_send.at[lax.rem(me + d, n)], second_out.at[me], zs_send.at[d], zs_recv.at[d], along(d)
        )

    def first_across(d, shift):
        source = lax.rem(me + n - d, n)
        other = lax.rem(my_win + shift, nwin)
        ref = first_send if d == 0 else first_out
        k = d * nwin + shift
        return remote(
            ref.at[source, other], first_x.at[shift - 1, source], xf_send.at[k], xf_recv.at[k], across(shift)
        )

    def second_across(d, shift):
        source = lax.rem(me + n - d, n)
        ref = second_send if d == 0 else second_out
        k = d * nwin + shift
        return remote(
            ref.at[source], second_x.at[shift - 1, source], xs_send.at[k], xs_recv.at[k], across(shift)
        )

    order = sorted(range(1, n), key=lambda d: min(d, n - d))
    for d in order:

        @pl.when(me + d < n)
        def _(d=d):
            first_to(d).start()

    own_first = pltpu.make_async_copy(first_send.at[me], first_out.at[me], own_sems.at[0])
    own_first.start()
    for shift in range(1, nwin):
        first_across(0, shift).start()

    @pl.when(me > 0)
    def _():
        to_left.wait_send()

    for d in order:

        @pl.when(me + d >= n)
        def _(d=d):
            first_to(d).start()

    @pl.when(me == n - 1)
    def _():
        spill_in[...] = jnp.zeros_like(spill_in)

    @pl.when(me < n - 1)
    def _():
        to_left.wait_recv()

    for d in order + [0]:
        o = lax.rem(me + d, n)
        total = second_local[o].astype(jnp.float32)
        for q in range(pairs_dev):
            total = total + spill_in[q].astype(jnp.float32) * mask[o, q : q + 1, :]
        second_send[o] = total.astype(jnp.bfloat16)
        if d:
            second_to(d).start()
    own_second = pltpu.make_async_copy(second_send.at[me], second_out.at[me], own_sems.at[1])
    own_second.start()
    for shift in range(1, nwin):
        second_across(0, shift).start()

    for d in order:
        first_to(d).wait_recv()
        for shift in range(1, nwin):
            first_across(d, shift).start()
    for d in order:
        second_to(d).wait_recv()
        for shift in range(1, nwin):
            second_across(d, shift).start()
    own_first.wait()
    own_second.wait()

    for d in order:
        first_to(d).wait_send()
        second_to(d).wait_send()
    for d in range(n):
        for shift in range(1, nwin):
            first_across(d, shift).wait()
            second_across(d, shift).wait()


def exchange(spill, first_send, second_local, mask):
    n, nwin, first_rows, bins = first_send.shape
    rows = second_local.shape[1]
    hbm = pl.BlockSpec(memory_space=pl.ANY)
    vmem = pl.BlockSpec(memory_space=pltpu.VMEM)
    dma = pltpu.SemaphoreType.DMA
    sent = jax.ShapeDtypeStruct
    return pl.pallas_call(
        functools.partial(exchange_kernel, n, nwin),
        in_specs=[hbm, hbm, vmem, vmem],
        out_specs=[hbm] * 4,
        out_shape=[
            sent(first_send.shape, jnp.bfloat16),
            sent(second_local.shape, jnp.bfloat16),
            sent((nwin - 1, n, first_rows, bins), jnp.bfloat16),
            sent((nwin - 1, n, rows, bins), jnp.bfloat16),
        ],
        scratch_shapes=[
            pltpu.VMEM(spill.shape, jnp.bfloat16),
            pltpu.VMEM(second_local.shape, jnp.bfloat16),
            dma((2,)),
            dma((n,)), dma((n,)), dma((n,)), dma((n,)),
            dma((n * nwin,)), dma((n * nwin,)), dma((n * nwin,)), dma((n * nwin,)),
            dma((2,)),
        ],
        compiler_params=pltpu.CompilerParams(
            collective_id=0, has_side_effects=True, vmem_limit_bytes=32 * MIB
        ),
        cost_estimate=pl.CostEstimate(flops=0, bytes_accessed=4 * MIB, transcendentals=0),
    )(spill, first_send, second_local, mask)


def tiles_kernel(meta_ref, pick_ref, *refs, nwin, win_dev, first_rows, width):
    firsts, seconds = refs[:nwin], refs[nwin : 2 * nwin]
    out_ref, left, right = refs[2 * nwin :]
    slots = pl.num_programs(0)
    slot = pl.program_id(0)
    windows = nwin * win_dev
    bins = out_ref.shape[4]
    filled = pick_ref[slots + slot]

    @pl.when(filled == 0)
    def _():
        out_ref[...] = jnp.zeros_like(out_ref)

    @pl.when(filled != 0)
    def _():
        def whitened(ends, rows, scale):
            real, imag = [], []
            for ref in ends:
                view = ref[...].reshape(2, win_dev, rows, bins).astype(jnp.float32)
                for w in range(win_dev):
                    real.append(view[0, w])
                    imag.append(view[1, w])
            power = sum(r * r + i * i for r, i in zip(real, imag)) * (1.0 / windows)
            gain = lax.rsqrt(power + eps_power) * scale
            return [r * gain for r in real], [i * gain for i in imag]

        real, imag = whitened(firsts, first_rows, 1.0 / windows)
        for w in range(windows):
            for term, value in enumerate((real[w] + imag[w], real[w], imag[w])):
                for part in range(bins // 128):
                    left[part, term * windows + w] = value[:, part * 128 : part * 128 + 128]
        real, imag = whitened(seconds, width, 1.0)
        for w in range(windows):
            right[w] = real[w]
            right[windows + w] = real[w] + imag[w]
            right[2 * windows + w] = real[w] - imag[w]

        tile = 16
        for lane in range(0, bins, 128):

            def columns(t, carry, lane=lane):
                start = pl.multiple_of(t * tile, tile)
                held = [
                    right[n, pl.ds(start, tile), lane : lane + 128] for n in range(3 * windows)
                ]

                def row(i, c):
                    total = []
                    for term in range(3):
                        acc = None
                        for w in range(windows):
                            n = term * windows + w
                            one = left[lane // 128, n, pl.ds(i, 1), :]
                            prod = jnp.broadcast_to(one, (tile, 128)) * held[n]
                            acc = prod if acc is None else acc + prod
                        total.append(acc)
                    out_ref[0, 0, i, pl.ds(start, tile), lane : lane + 128] = (
                        total[0] - total[2]
                    ).astype(jnp.bfloat16)
                    out_ref[1, 0, i, pl.ds(start, tile), lane : lane + 128] = (
                        total[0] - total[1]
                    ).astype(jnp.bfloat16)
                    return c

                lax.fori_loop(0, first_rows, row, 0, unroll=8)
                return carry

            lax.fori_loop(0, width // tile, columns, 0)


def tiles(meta, pick, first_in, second_in, first_x, second_x, slots, win_dev, width):
    nwin, first_in_rows, bins = first_in.shape[1:]
    first_rows = first_in_rows // (2 * win_dev)
    whole = second_in.shape[1]
    shape = (2, slots, first_rows, width, bins)
    first_specs = [
        pl.BlockSpec((1, 1, first_in_rows, bins), lambda s, m, p: (p[s], m[2], 0, 0))
    ] + [
        pl.BlockSpec((1, 1, first_in_rows, bins), lambda s, m, p, k=k: (k, p[s], 0, 0))
        for k in range(nwin - 1)
    ]
    second_specs = [pl.BlockSpec((1, whole, bins), lambda s, m, p: (p[s], 0, 0))] + [
        pl.BlockSpec((1, 1, whole, bins), lambda s, m, p, k=k: (k, p[s], 0, 0))
        for k in range(nwin - 1)
    ]
    windows = nwin * win_dev
    return pl.pallas_call(
        functools.partial(
            tiles_kernel, nwin=nwin, win_dev=win_dev, first_rows=first_rows, width=width
        ),
        grid_spec=pltpu.PrefetchScalarGridSpec(
            num_scalar_prefetch=2,
            grid=(slots,),
            in_specs=first_specs + second_specs,
            out_specs=pl.BlockSpec(
                (2, 1, first_rows, width, bins), lambda s, m, p: (0, s, 0, 0, 0)
            ),
            scratch_shapes=[
                pltpu.VMEM((bins // 128, 3 * windows, first_rows, 128), jnp.float32),
                pltpu.VMEM((3 * windows, width, bins), jnp.float32),
            ],
        ),
        out_shape=jax.ShapeDtypeStruct(shape, jnp.bfloat16),
        compiler_params=pltpu.CompilerParams(vmem_limit_bytes=48 * MIB),
        cost_estimate=pl.CostEstimate(
            flops=16 * windows * math.prod(shape), bytes_accessed=12 * MIB, transcendentals=0
        ),
    )(meta, pick, first_in, *[first_x] * (nwin - 1), second_in, *[second_x] * (nwin - 1))


def shards(table, traces, block_members, pair_blocks, pair_owner):
    width = block_members.shape[1]
    local_rows, win_dev, samples = traces.shape
    owners = lax.axis_size("blk")
    nwin = lax.axis_size("win")
    slots = 2 * PAIR_DEV
    meta = jnp.stack([lax.axis_index(name) for name in ("blk", "frq", "win")]).astype(jnp.int32)
    spill, first_send, second_local, mask, pick = spectra(
        meta,
        pair_blocks.reshape(-1),
        pair_owner.reshape(-1),
        block_members,
        traces.reshape(local_rows * win_dev, samples),
        table,
        owners,
        nwin,
        win_dev,
        slots,
    )
    arrived = exchange(spill, first_send, second_local, mask)
    return tiles(meta, pick, *arrived, slots, win_dev, width)


def solution(mesh):
    placed = (
        P(("parts", "blk"), "win", None),
        P(("parts", "blk"), None),
        P("parts", None),
        P("parts", None),
    )

    def whole(traces, block_members, pair_blocks, pair_owner):
        table = jnp.asarray(dft_tables(traces.shape[2], mesh.shape["frq"]))
        return jax.shard_map(
            shards,
            mesh=mesh,
            in_specs=(P(None, None, None),) + placed,
            out_specs=P(None, ("parts", "blk"), "win", None, "frq"),
            check_vma=False,
        )(table, traces, block_members, pair_blocks, pair_owner)

    return whole
```

```python
import functools
import math

import jax
import jax.numpy as jnp
import numpy as np
from jax import lax
from jax.experimental import pallas as pl
from jax.experimental.pallas import tpu as pltpu
from jax.sharding import PartitionSpec as P

FREQS = 512
PAIR_DEV = 2
CHUNKS = 4

eps_time = 1e-05
eps_power = 1e-06
MIB = 1024 * 1024


def dft_tables(samples, parts):
    bins_dev = FREQS // parts
    t = np.arange(samples, dtype=np.int64)[:, None]
    k = np.arange(1, FREQS + 1, dtype=np.int64)[None, :]
    angles = (t * k % samples).astype(np.float32) * np.float32(2.0 * math.pi / samples)
    cos = np.cos(angles.astype(np.float64)).reshape(samples, parts, bins_dev)
    sin = np.sin(angles.astype(np.float64)).reshape(samples, parts, bins_dev)
    table = np.concatenate([cos, -sin], axis=2).transpose(1, 0, 2)
    return table.astype(np.float32).astype(jnp.bfloat16)


def spectra_kernel(
    meta_ref, blocks_ref, owner_ref, members_ref, x_ref, table_ref,
    spill, first_send, second_local, mask, pick, spectra, perm, *, row_tile, win_dev,
):
    step = pl.program_id(0)
    block_count, width = members_ref.shape
    owners, nwin, first_rows, bins = first_send.shape
    pairs_dev = spill.shape[0]
    slots = pick.shape[0] // 2
    x = x_ref[...].astype(jnp.float32)
    centre = x - jnp.mean(x, axis=1, keepdims=True)
    spread = jnp.mean(centre * centre, axis=1, keepdims=True)
    normal = (centre * lax.rsqrt(spread + eps_time)).astype(jnp.bfloat16)
    product = jnp.dot(normal, table_ref[0], preferred_element_type=jnp.float32)
    start = pl.multiple_of(step * row_tile, row_tile)
    spectra[pl.ds(start, row_tile), :] = product.astype(jnp.bfloat16)

    @pl.when(step == pl.num_programs(0) - 1)
    def _():
        me = meta_ref[0]
        rows = spectra.shape[0]
        chunk = win_dev * width
        half = width // nwin
        local = members_ref[...] % (rows // win_dev) * win_dev
        place = jnp.concatenate([local + w for w in range(win_dev)], axis=1)
        for block in range(block_count):
            row = lax.broadcasted_iota(jnp.int32, (rows, chunk), 0)
            onehot = jnp.where(row == place[block : block + 1, :], 1.0, 0.0).astype(jnp.bfloat16)
            perm[block] = lax.dot_general(
                onehot, spectra[...], (((0,), (0,)), ((), ())), preferred_element_type=jnp.float32
            ).astype(jnp.bfloat16)

        def whole_block(out, n, block):
            inside = (block >= 0) & (block < block_count)

            @pl.when(inside)
            def _():
                for part in range(2):
                    out[n, part * chunk : part * chunk + chunk, :] = perm[
                        block, :, part * bins : part * bins + bins
                    ]

            @pl.when(jnp.logical_not(inside))
            def _():
                out[n] = jnp.zeros(out.shape[1:], out.dtype)

        def halves(n, block):
            @pl.when(block >= 0)
            def _():
                for h in range(nwin):
                    for part in range(2):
                        for w in range(win_dev):
                            at = (part * win_dev + w) * half
                            first_send[n, h, at : at + half, :] = perm[
                                block,
                                w * width + h * half : w * width + h * half + half,
                                part * bins : part * bins + bins,
                            ]

            @pl.when(block < 0)
            def _():
                first_send[n] = jnp.zeros(first_send.shape[1:], first_send.dtype)

        before = jnp.maximum(me - 1, 0) * pairs_dev
        for q in range(pairs_dev):
            whole_block(spill, q, blocks_ref[(before + q) * 2 + 1] - me * block_count)

        def to_owner(o, carry):
            first, second = jnp.int32(-1), jnp.int32(-1)
            for q in range(pairs_dev):
                pair = me * pairs_dev + q
                hit = owner_ref[pair] == o
                first_end = blocks_ref[2 * pair] - me * block_count
                second_end = blocks_ref[2 * pair + 1] - me * block_count
                first = jnp.where(hit, first_end, first)
                second = jnp.where(hit, second_end, second)
                value = jnp.where(hit & (second_end >= block_count), 1.0, 0.0)
                mask[o, q : q + 1, :] = jnp.full((1, bins), value, jnp.float32)
            halves(o, first)
            whole_block(second_local, o, second)
            return carry

        lax.fori_loop(0, owners, to_owner, 0)

        for n in range(2 * slots):
            pick[n] = 0

        def from_group(g, rank):
            hit = owner_ref[g * pairs_dev] == me
            for q in range(1, pairs_dev):
                hit = hit | (owner_ref[g * pairs_dev + q] == me)

            @pl.when(hit & (rank < slots))
            def _():
                pick[rank] = g
                pick[slots + rank] = 1

            return rank + hit.astype(jnp.int32)

        lax.fori_loop(0, owners, from_group, jnp.int32(0))


def spectra(meta, pair_blocks, pair_owner, members, x, table, owners, nwin, win_dev, slots):
    rows, samples = x.shape
    cols = table.shape[2]
    bins = cols // 2
    block_count, width = members.shape
    chunk = win_dev * width
    row_tile = rows // 2
    whole = 2 * chunk
    shapes = [
        jax.ShapeDtypeStruct((PAIR_DEV, whole, bins), jnp.bfloat16),
        jax.ShapeDtypeStruct((owners, nwin, whole // nwin, bins), jnp.bfloat16),
        jax.ShapeDtypeStruct((owners, whole, bins), jnp.bfloat16),
        jax.ShapeDtypeStruct((owners, PAIR_DEV, bins), jnp.float32),
        jax.ShapeDtypeStruct((2 * slots,), jnp.int32),
    ]

    def fixed(shape):
        return pl.BlockSpec(shape, lambda i, *_: (0,) * len(shape))

    return pl.pallas_call(
        functools.partial(spectra_kernel, row_tile=row_tile, win_dev=win_dev),
        grid_spec=pltpu.PrefetchScalarGridSpec(
            num_scalar_prefetch=3,
            grid=(rows // row_tile,),
            in_specs=[
                fixed(members.shape),
                pl.BlockSpec((row_tile, samples), lambda i, *_: (i, 0)),
                pl.BlockSpec((1, samples, cols), lambda i, m, *_: (m[1], 0, 0)),
            ],
            out_specs=[fixed(s.shape) for s in shapes[:-1]]
            + [pl.BlockSpec(memory_space=pltpu.SMEM)],
            scratch_shapes=[
                pltpu.VMEM((rows, cols), jnp.bfloat16),
                pltpu.VMEM((block_count, chunk, cols), jnp.bfloat16),
            ],
        ),
        out_shape=shapes,
        compiler_params=pltpu.CompilerParams(vmem_limit_bytes=48 * MIB),
        cost_estimate=pl.CostEstimate(
            flops=2 * rows * samples * cols, bytes_accessed=8 * MIB, transcendentals=rows
        ),
    )(meta, pair_blocks, pair_owner, members, x, table)


def exchange_kernel(
    n, nwin, spill, first_send, second_local, mask,
    first_out, second_out, first_x, second_x,
    spill_in, second_send,
    spill_sems, zf_send, zf_recv, zs_send, zs_recv, xf_send, xf_recv, xs_send, xs_recv, own_sems,
):
    me = lax.axis_index("blk")
    my_win = lax.axis_index("win")
    pairs_dev = spill.shape[0]

    def along(d):
        return {"blk": lax.rem(me + d, n)}

    def across(shift):
        return {"win": lax.rem(my_win + shift, nwin)}

    def remote(src, dst, send, recv, device):
        return pltpu.make_async_remote_copy(
            src_ref=src, dst_ref=dst, send_sem=send, recv_sem=recv,
            device_id=device, device_id_type=pl.DeviceIdType.MESH,
        )

    barrier = pltpu.get_barrier_semaphore()
    for d in range(1, n):
        pl.semaphore_signal(barrier, inc=1, device_id=along(d), device_id_type=pl.DeviceIdType.MESH)
    for s in range(1, nwin):
        pl.semaphore_signal(barrier, inc=1, device_id=across(s), device_id_type=pl.DeviceIdType.MESH)
    pl.semaphore_wait(barrier, n + nwin - 2)

    to_left = remote(spill, spill_in, spill_sems.at[0], spill_sems.at[1], along(n - 1))

    @pl.when(me > 0)
    def _():
        to_left.start()

    def first_to(d):
        return remote(
            first_send.at[lax.rem(me + d, n)], first_out.at[me], zf_send.at[d], zf_recv.at[d], along(d)
        )

    piece = second_send.shape[1] // CHUNKS

    def second_to(d, c):
        rows = pl.ds(c * piece, piece)
        k = d * CHUNKS + c
        return remote(
            second_send.at[lax.rem(me + d, n), rows], second_out.at[me, rows],
            zs_send.at[k], zs_recv.at[k], along(d),
        )

    def first_across(d, shift):
        source = lax.rem(me + n - d, n)
        other = lax.rem(my_win + shift, nwin)
        ref = first_send if d == 0 else first_out
        k = d * nwin + shift
        return remote(
            ref.at[source, other], first_x.at[shift - 1, source], xf_send.at[k], xf_recv.at[k], across(shift)
        )

    def second_across(d, c, shift):
        source = lax.rem(me + n - d, n)
        ref = second_send if d == 0 else second_out
        rows = pl.ds(c * piece, piece)
        k = (d * CHUNKS + c) * nwin + shift
        return remote(
            ref.at[source, rows], second_x.at[shift - 1, source, rows],
            xs_send.at[k], xs_recv.at[k], across(shift),
        )

    order = sorted(range(1, n), key=lambda d: min(d, n - d))
    for d in order:

        @pl.when(me + d < n)
        def _(d=d):
            first_to(d).start()

    own_first = pltpu.make_async_copy(first_send.at[me], first_out.at[me], own_sems.at[0])
    own_first.start()
    for shift in range(1, nwin):
        first_across(0, shift).start()

    @pl.when(me > 0)
    def _():
        to_left.wait_send()

    for d in order:

        @pl.when(me + d >= n)
        def _(d=d):
            first_to(d).start()

    @pl.when(me == n - 1)
    def _():
        spill_in[...] = jnp.zeros_like(spill_in)

    @pl.when(me < n - 1)
    def _():
        to_left.wait_recv()

    for d in order + [0]:
        o = lax.rem(me + d, n)
        total = second_local[o].astype(jnp.float32)
        for q in range(pairs_dev):
            total = total + spill_in[q].astype(jnp.float32) * mask[o, q : q + 1, :]
        second_send[o] = total.astype(jnp.bfloat16)
    for c in range(CHUNKS):
        for d in order:
            second_to(d, c).start()
    own_second = pltpu.make_async_copy(second_send.at[me], second_out.at[me], own_sems.at[1])
    own_second.start()
    for shift in range(1, nwin):
        for c in range(CHUNKS):
            second_across(0, c, shift).start()

    for d in order:
        first_to(d).wait_recv()
        for shift in range(1, nwin):
            first_across(d, shift).start()
    for c in range(CHUNKS):
        for d in order:
            second_to(d, c).wait_recv()
            for shift in range(1, nwin):
                second_across(d, c, shift).start()
    own_first.wait()
    own_second.wait()

    for d in order:
        first_to(d).wait_send()
        for c in range(CHUNKS):
            second_to(d, c).wait_send()
    for d in range(n):
        for shift in range(1, nwin):
            first_across(d, shift).wait()
            for c in range(CHUNKS):
                second_across(d, c, shift).wait()


def exchange(spill, first_send, second_local, mask):
    n, nwin, first_rows, bins = first_send.shape
    rows = second_local.shape[1]
    hbm = pl.BlockSpec(memory_space=pl.ANY)
    vmem = pl.BlockSpec(memory_space=pltpu.VMEM)
    dma = pltpu.SemaphoreType.DMA
    sent = jax.ShapeDtypeStruct
    return pl.pallas_call(
        functools.partial(exchange_kernel, n, nwin),
        in_specs=[hbm, hbm, vmem, vmem],
        out_specs=[hbm] * 4,
        out_shape=[
            sent(first_send.shape, jnp.bfloat16),
            sent(second_local.shape, jnp.bfloat16),
            sent((nwin - 1, n, first_rows, bins), jnp.bfloat16),
            sent((nwin - 1, n, rows, bins), jnp.bfloat16),
        ],
        scratch_shapes=[
            pltpu.VMEM(spill.shape, jnp.bfloat16),
            pltpu.VMEM(second_local.shape, jnp.bfloat16),
            dma((2,)),
            dma((n,)), dma((n,)), dma((n * CHUNKS,)), dma((n * CHUNKS,)),
            dma((n * nwin,)), dma((n * nwin,)),
            dma((n * nwin * CHUNKS,)), dma((n * nwin * CHUNKS,)),
            dma((2,)),
        ],
        compiler_params=pltpu.CompilerParams(
            collective_id=0, has_side_effects=True, vmem_limit_bytes=32 * MIB
        ),
        cost_estimate=pl.CostEstimate(flops=0, bytes_accessed=4 * MIB, transcendentals=0),
    )(spill, first_send, second_local, mask)


def tiles_kernel(meta_ref, pick_ref, *refs, nwin, win_dev, first_rows, width):
    firsts, seconds = refs[:nwin], refs[nwin : 2 * nwin]
    out_ref, left, right = refs[2 * nwin :]
    slots = pl.num_programs(0)
    slot = pl.program_id(0)
    share = pl.program_id(1)
    some_rows = out_ref.shape[2]
    windows = nwin * win_dev
    bins = out_ref.shape[4]
    filled = pick_ref[slots + slot]

    @pl.when(filled == 0)
    def _():
        out_ref[...] = jnp.zeros_like(out_ref)

    @pl.when((filled != 0) & (share == 0))
    def _():
        def whitened(ends, rows, scale):
            real, imag = [], []
            for ref in ends:
                view = ref[...].reshape(2, win_dev, rows, bins).astype(jnp.float32)
                for w in range(win_dev):
                    real.append(view[0, w])
                    imag.append(view[1, w])
            power = sum(r * r + i * i for r, i in zip(real, imag)) * (1.0 / windows)
            gain = lax.rsqrt(power + eps_power) * scale
            return [r * gain for r in real], [i * gain for i in imag]

        real, imag = whitened(firsts, first_rows, 1.0 / windows)
        for w in range(windows):
            for term, value in enumerate((real[w] + imag[w], real[w], imag[w])):
                for part in range(bins // 128):
                    left[part, term * windows + w] = value[:, part * 128 : part * 128 + 128]
        real, imag = whitened(seconds, width, 1.0)
        for w in range(windows):
            right[w] = real[w]
            right[windows + w] = real[w] + imag[w]
            right[2 * windows + w] = real[w] - imag[w]

    @pl.when(filled != 0)
    def _():
        tile = 16
        for lane in range(0, bins, 128):

            def columns(t, carry, lane=lane):
                start = pl.multiple_of(t * tile, tile)
                held = [
                    right[n, pl.ds(start, tile), lane : lane + 128] for n in range(3 * windows)
                ]

                def row(i, c):
                    total = []
                    for term in range(3):
                        acc = None
                        for w in range(windows):
                            n = term * windows + w
                            one = left[lane // 128, n, pl.ds(share * some_rows + i, 1), :]
                            prod = jnp.broadcast_to(one, (tile, 128)) * held[n]
                            acc = prod if acc is None else acc + prod
                        total.append(acc)
                    out_ref[0, 0, i, pl.ds(start, tile), lane : lane + 128] = (
                        total[0] - total[2]
                    ).astype(jnp.bfloat16)
                    out_ref[1, 0, i, pl.ds(start, tile), lane : lane + 128] = (
                        total[0] - total[1]
                    ).astype(jnp.bfloat16)
                    return c

                lax.fori_loop(0, some_rows, row, 0, unroll=8)
                return carry

            lax.fori_loop(0, width // tile, columns, 0)


def tiles(meta, pick, first_in, second_in, first_x, second_x, slots, win_dev, width):
    nwin, first_in_rows, bins = first_in.shape[1:]
    first_rows = first_in_rows // (2 * win_dev)
    whole = second_in.shape[1]
    shape = (2, slots, first_rows, width, bins)
    first_specs = [
        pl.BlockSpec((1, 1, first_in_rows, bins), lambda s, t, m, p: (p[s], m[2], 0, 0))
    ] + [
        pl.BlockSpec((1, 1, first_in_rows, bins), lambda s, t, m, p, k=k: (k, p[s], 0, 0))
        for k in range(nwin - 1)
    ]
    second_specs = [pl.BlockSpec((1, whole, bins), lambda s, t, m, p: (p[s], 0, 0))] + [
        pl.BlockSpec((1, 1, whole, bins), lambda s, t, m, p, k=k: (k, p[s], 0, 0))
        for k in range(nwin - 1)
    ]
    windows = nwin * win_dev
    return pl.pallas_call(
        functools.partial(
            tiles_kernel, nwin=nwin, win_dev=win_dev, first_rows=first_rows, width=width
        ),
        grid_spec=pltpu.PrefetchScalarGridSpec(
            num_scalar_prefetch=2,
            grid=(slots, 2),
            in_specs=first_specs + second_specs,
            out_specs=pl.BlockSpec(
                (2, 1, first_rows // 2, width, bins), lambda s, t, m, p: (0, s, t, 0, 0)
            ),
            scratch_shapes=[
                pltpu.VMEM((bins // 128, 3 * windows, first_rows, 128), jnp.float32),
                pltpu.VMEM((3 * windows, width, bins), jnp.float32),
            ],
        ),
        out_shape=jax.ShapeDtypeStruct(shape, jnp.bfloat16),
        compiler_params=pltpu.CompilerParams(vmem_limit_bytes=48 * MIB),
        cost_estimate=pl.CostEstimate(
            flops=16 * windows * math.prod(shape), bytes_accessed=12 * MIB, transcendentals=0
        ),
    )(meta, pick, first_in, *[first_x] * (nwin - 1), second_in, *[second_x] * (nwin - 1))


def shards(table, traces, block_members, pair_blocks, pair_owner):
    width = block_members.shape[1]
    local_rows, win_dev, samples = traces.shape
    owners = lax.axis_size("blk")
    nwin = lax.axis_size("win")
    slots = 2 * PAIR_DEV
    meta = jnp.stack([lax.axis_index(name) for name in ("blk", "frq", "win")]).astype(jnp.int32)
    spill, first_send, second_local, mask, pick = spectra(
        meta,
        pair_blocks.reshape(-1),
        pair_owner.reshape(-1),
        block_members,
        traces.reshape(local_rows * win_dev, samples),
        table,
        owners,
        nwin,
        win_dev,
        slots,
    )
    arrived = exchange(spill, first_send, second_local, mask)
    return tiles(meta, pick, *arrived, slots, win_dev, width)


def solution(mesh):
    placed = (
        P(("parts", "blk"), "win", None),
        P(("parts", "blk"), None),
        P("parts", None),
        P("parts", None),
    )

    def whole(traces, block_members, pair_blocks, pair_owner):
        table = jnp.asarray(dft_tables(traces.shape[2], mesh.shape["frq"]))
        return jax.shard_map(
            shards,
            mesh=mesh,
            in_specs=(P(None, None, None),) + placed,
            out_specs=P(None, ("parts", "blk"), "win", None, "frq"),
            check_vma=False,
        )(table, traces, block_members, pair_blocks, pair_owner)

    return whole
```

```python
import functools
import math

import jax
import jax.numpy as jnp
import numpy as np
from jax import lax
from jax.experimental import pallas as pl
from jax.experimental.pallas import tpu as pltpu
from jax.sharding import PartitionSpec as P

FREQS = 512
PAIR_DEV = 2

eps_time = 1e-05
eps_power = 1e-06
MIB = 1024 * 1024


def dft_tables(samples, parts):
    bins_dev = FREQS // parts
    t = np.arange(samples, dtype=np.int64)[:, None]
    k = np.arange(1, FREQS + 1, dtype=np.int64)[None, :]
    angles = (t * k % samples).astype(np.float32) * np.float32(2.0 * math.pi / samples)
    cos = np.cos(angles.astype(np.float64)).reshape(samples, parts, bins_dev)
    sin = np.sin(angles.astype(np.float64)).reshape(samples, parts, bins_dev)
    table = np.concatenate([cos, -sin], axis=2).transpose(1, 0, 2)
    return table.astype(np.float32).astype(jnp.bfloat16)


def spectra_kernel(
    meta_ref, blocks_ref, owner_ref, members_ref, x_ref, table_ref,
    spill, first_send, second_local, mask, pick, spectra, perm, *, row_tile, win_dev,
):
    step = pl.program_id(0)
    block_count, width = members_ref.shape
    owners, nwin, first_rows, bins = first_send.shape
    pairs_dev = spill.shape[0]
    slots = pick.shape[0] // 2
    x = x_ref[...].astype(jnp.float32)
    centre = x - jnp.mean(x, axis=1, keepdims=True)
    spread = jnp.mean(centre * centre, axis=1, keepdims=True)
    normal = (centre * lax.rsqrt(spread + eps_time)).astype(jnp.bfloat16)
    product = jnp.dot(normal, table_ref[0], preferred_element_type=jnp.float32)
    start = pl.multiple_of(step * row_tile, row_tile)
    spectra[pl.ds(start, row_tile), :] = product.astype(jnp.bfloat16)

    @pl.when(step == pl.num_programs(0) - 1)
    def _():
        me = meta_ref[0]
        rows = spectra.shape[0]
        chunk = win_dev * width
        half = width // nwin
        local = members_ref[...] % (rows // win_dev) * win_dev
        place = jnp.concatenate([local + w for w in range(win_dev)], axis=1)
        for block in range(block_count):
            row = lax.broadcasted_iota(jnp.int32, (rows, chunk), 0)
            onehot = jnp.where(row == place[block : block + 1, :], 1.0, 0.0).astype(jnp.bfloat16)
            perm[block] = lax.dot_general(
                onehot, spectra[...], (((0,), (0,)), ((), ())), preferred_element_type=jnp.float32
            ).astype(jnp.bfloat16)

        def whole_block(out, n, block):
            inside = (block >= 0) & (block < block_count)

            @pl.when(inside)
            def _():
                for part in range(2):
                    out[n, part * chunk : part * chunk + chunk, :] = perm[
                        block, :, part * bins : part * bins + bins
                    ]

            @pl.when(jnp.logical_not(inside))
            def _():
                out[n] = jnp.zeros(out.shape[1:], out.dtype)

        def halves(n, block):
            @pl.when(block >= 0)
            def _():
                for h in range(nwin):
                    for part in range(2):
                        for w in range(win_dev):
                            at = (part * win_dev + w) * half
                            first_send[n, h, at : at + half, :] = perm[
                                block,
                                w * width + h * half : w * width + h * half + half,
                                part * bins : part * bins + bins,
                            ]

            @pl.when(block < 0)
            def _():
                first_send[n] = jnp.zeros(first_send.shape[1:], first_send.dtype)

        before = jnp.maximum(me - 1, 0) * pairs_dev
        for q in range(pairs_dev):
            whole_block(spill, q, blocks_ref[(before + q) * 2 + 1] - me * block_count)

        def to_owner(o, carry):
            first, second = jnp.int32(-1), jnp.int32(-1)
            for q in range(pairs_dev):
                pair = me * pairs_dev + q
                hit = owner_ref[pair] == o
                first_end = blocks_ref[2 * pair] - me * block_count
                second_end = blocks_ref[2 * pair + 1] - me * block_count
                first = jnp.where(hit, first_end, first)
                second = jnp.where(hit, second_end, second)
                value = jnp.where(hit & (second_end >= block_count), 1.0, 0.0)
                mask[o, q : q + 1, :] = jnp.full((1, bins), value, jnp.float32)
            halves(o, first)
            whole_block(second_local, o, second)
            return carry

        lax.fori_loop(0, owners, to_owner, 0)

        for n in range(2 * slots):
            pick[n] = 0

        def from_group(g, rank):
            hit = owner_ref[g * pairs_dev] == me
            for q in range(1, pairs_dev):
                hit = hit | (owner_ref[g * pairs_dev + q] == me)

            @pl.when(hit & (rank < slots))
            def _():
                pick[rank] = g
                pick[slots + rank] = 1

            return rank + hit.astype(jnp.int32)

        lax.fori_loop(0, owners, from_group, jnp.int32(0))


def spectra(meta, pair_blocks, pair_owner, members, x, table, owners, nwin, win_dev, slots):
    rows, samples = x.shape
    cols = table.shape[2]
    bins = cols // 2
    block_count, width = members.shape
    chunk = win_dev * width
    row_tile = rows // 4
    whole = 2 * chunk
    shapes = [
        jax.ShapeDtypeStruct((PAIR_DEV, whole, bins), jnp.bfloat16),
        jax.ShapeDtypeStruct((owners, nwin, whole // nwin, bins), jnp.bfloat16),
        jax.ShapeDtypeStruct((owners, whole, bins), jnp.bfloat16),
        jax.ShapeDtypeStruct((owners, PAIR_DEV, bins), jnp.float32),
        jax.ShapeDtypeStruct((2 * slots,), jnp.int32),
    ]

    def fixed(shape):
        return pl.BlockSpec(shape, lambda i, *_: (0,) * len(shape))

    return pl.pallas_call(
        functools.partial(spectra_kernel, row_tile=row_tile, win_dev=win_dev),
        grid_spec=pltpu.PrefetchScalarGridSpec(
            num_scalar_prefetch=3,
            grid=(rows // row_tile,),
            in_specs=[
                fixed(members.shape),
                pl.BlockSpec((row_tile, samples), lambda i, *_: (i, 0)),
                pl.BlockSpec((1, samples, cols), lambda i, m, *_: (m[1], 0, 0)),
            ],
            out_specs=[fixed(s.shape) for s in shapes[:-1]]
            + [pl.BlockSpec(memory_space=pltpu.SMEM)],
            scratch_shapes=[
                pltpu.VMEM((rows, cols), jnp.bfloat16),
                pltpu.VMEM((block_count, chunk, cols), jnp.bfloat16),
            ],
        ),
        out_shape=shapes,
        compiler_params=pltpu.CompilerParams(vmem_limit_bytes=48 * MIB),
        cost_estimate=pl.CostEstimate(
            flops=2 * rows * samples * cols, bytes_accessed=8 * MIB, transcendentals=rows
        ),
    )(meta, pair_blocks, pair_owner, members, x, table)


def exchange_kernel(
    n, nwin, spill, first_send, second_local, mask,
    first_out, second_out, first_x, second_x,
    spill_in, second_send,
    spill_sems, zf_send, zf_recv, zs_send, zs_recv, xf_send, xf_recv, xs_send, xs_recv, own_sems,
):
    me = lax.axis_index("blk")
    my_win = lax.axis_index("win")
    pairs_dev = spill.shape[0]

    def along(d):
        return {"blk": lax.rem(me + d, n)}

    def across(shift):
        return {"win": lax.rem(my_win + shift, nwin)}

    def remote(src, dst, send, recv, device):
        return pltpu.make_async_remote_copy(
            src_ref=src, dst_ref=dst, send_sem=send, recv_sem=recv,
            device_id=device, device_id_type=pl.DeviceIdType.MESH,
        )

    barrier = pltpu.get_barrier_semaphore()
    for d in range(1, n):
        pl.semaphore_signal(barrier, inc=1, device_id=along(d), device_id_type=pl.DeviceIdType.MESH)
    for s in range(1, nwin):
        pl.semaphore_signal(barrier, inc=1, device_id=across(s), device_id_type=pl.DeviceIdType.MESH)
    pl.semaphore_wait(barrier, n + nwin - 2)

    to_left = remote(spill, spill_in, spill_sems.at[0], spill_sems.at[1], along(n - 1))

    @pl.when(me > 0)
    def _():
        to_left.start()

    def first_to(d):
        return remote(
            first_send.at[lax.rem(me + d, n)], first_out.at[me], zf_send.at[d], zf_recv.at[d], along(d)
        )

    def second_to(d):
        return remote(
            second_send.at[lax.rem(me + d, n)], second_out.at[me], zs_send.at[d], zs_recv.at[d], along(d)
        )

    def first_across(d, shift):
        source = lax.rem(me + n - d, n)
        other = lax.rem(my_win + shift, nwin)
        ref = first_send if d == 0 else first_out
        k = d * nwin + shift
        return remote(
            ref.at[source, other], first_x.at[shift - 1, source], xf_send.at[k], xf_recv.at[k], across(shift)
        )

    def second_across(d, shift):
        source = lax.rem(me + n - d, n)
        ref = second_send if d == 0 else second_out
        k = d * nwin + shift
        return remote(
            ref.at[source], second_x.at[shift - 1, source], xs_send.at[k], xs_recv.at[k], across(shift)
        )

    order = sorted(range(1, n), key=lambda d: min(d, n - d))
    for d in order[::-1]:
        first_to(d).start()
    own_first = pltpu.make_async_copy(first_send.at[me], first_out.at[me], own_sems.at[0])
    own_first.start()
    for shift in range(1, nwin):
        first_across(0, shift).start()

    @pl.when(me == n - 1)
    def _():
        spill_in[...] = jnp.zeros_like(spill_in)

    @pl.when(me < n - 1)
    def _():
        to_left.wait_recv()

    for d in order[::-1] + [0]:
        o = lax.rem(me + d, n)
        total = second_local[o].astype(jnp.float32)
        for q in range(pairs_dev):
            total = total + spill_in[q].astype(jnp.float32) * mask[o, q : q + 1, :]
        second_send[o] = total.astype(jnp.bfloat16)
        if d:
            second_to(d).start()
    own_second = pltpu.make_async_copy(second_send.at[me], second_out.at[me], own_sems.at[1])
    own_second.start()
    for shift in range(1, nwin):
        second_across(0, shift).start()

    for d in order:
        first_to(d).wait_recv()
        for shift in range(1, nwin):
            first_across(d, shift).start()
    for d in order:
        second_to(d).wait_recv()
        for shift in range(1, nwin):
            second_across(d, shift).start()
    own_first.wait()
    own_second.wait()

    @pl.when(me > 0)
    def _():
        to_left.wait_send()

    for d in order:
        first_to(d).wait_send()
        second_to(d).wait_send()
    for d in range(n):
        for shift in range(1, nwin):
            first_across(d, shift).wait()
            second_across(d, shift).wait()


def exchange(spill, first_send, second_local, mask):
    n, nwin, first_rows, bins = first_send.shape
    rows = second_local.shape[1]
    hbm = pl.BlockSpec(memory_space=pl.ANY)
    vmem = pl.BlockSpec(memory_space=pltpu.VMEM)
    dma = pltpu.SemaphoreType.DMA
    sent = jax.ShapeDtypeStruct
    return pl.pallas_call(
        functools.partial(exchange_kernel, n, nwin),
        in_specs=[hbm, hbm, vmem, vmem],
        out_specs=[hbm] * 4,
        out_shape=[
            sent(first_send.shape, jnp.bfloat16),
            sent(second_local.shape, jnp.bfloat16),
            sent((nwin - 1, n, first_rows, bins), jnp.bfloat16),
            sent((nwin - 1, n, rows, bins), jnp.bfloat16),
        ],
        scratch_shapes=[
            pltpu.VMEM(spill.shape, jnp.bfloat16),
            pltpu.VMEM(second_local.shape, jnp.bfloat16),
            dma((2,)),
            dma((n,)), dma((n,)), dma((n,)), dma((n,)),
            dma((n * nwin,)), dma((n * nwin,)), dma((n * nwin,)), dma((n * nwin,)),
            dma((2,)),
        ],
        compiler_params=pltpu.CompilerParams(
            collective_id=0, has_side_effects=True, vmem_limit_bytes=32 * MIB
        ),
        cost_estimate=pl.CostEstimate(flops=0, bytes_accessed=4 * MIB, transcendentals=0),
    )(spill, first_send, second_local, mask)


def tiles_kernel(meta_ref, pick_ref, *refs, nwin, win_dev, first_rows, width):
    firsts, seconds = refs[:nwin], refs[nwin : 2 * nwin]
    out_ref, left, right = refs[2 * nwin :]
    slots = pl.num_programs(0)
    slot = pl.program_id(0)
    windows = nwin * win_dev
    bins = out_ref.shape[4]
    filled = pick_ref[slots + slot]

    @pl.when(filled == 0)
    def _():
        out_ref[...] = jnp.zeros_like(out_ref)

    @pl.when(filled != 0)
    def _():
        def whitened(ends, rows, scale):
            real, imag = [], []
            for ref in ends:
                view = ref[...].reshape(2, win_dev, rows, bins).astype(jnp.float32)
                for w in range(win_dev):
                    real.append(view[0, w])
                    imag.append(view[1, w])
            power = sum(r * r + i * i for r, i in zip(real, imag)) * (1.0 / windows)
            gain = lax.rsqrt(power + eps_power) * scale
            return [r * gain for r in real], [i * gain for i in imag]

        real, imag = whitened(firsts, first_rows, 1.0 / windows)
        for w in range(windows):
            for term, value in enumerate((real[w] + imag[w], real[w], imag[w])):
                for part in range(bins // 128):
                    left[part, term * windows + w] = value[:, part * 128 : part * 128 + 128]
        real, imag = whitened(seconds, width, 1.0)
        for w in range(windows):
            right[w] = real[w]
            right[windows + w] = real[w] + imag[w]
            right[2 * windows + w] = real[w] - imag[w]

        tile = 16
        for lane in range(0, bins, 128):

            def columns(t, carry, lane=lane):
                start = pl.multiple_of(t * tile, tile)
                held = [
                    right[n, pl.ds(start, tile), lane : lane + 128] for n in range(3 * windows)
                ]

                def row(i, c):
                    total = []
                    for term in range(3):
                        acc = None
                        for w in range(windows):
                            n = term * windows + w
                            one = left[lane // 128, n, pl.ds(i, 1), :]
                            prod = jnp.broadcast_to(one, (tile, 128)) * held[n]
                            acc = prod if acc is None else acc + prod
                        total.append(acc)
                    out_ref[0, 0, i, pl.ds(start, tile), lane : lane + 128] = (
                        total[0] - total[2]
                    ).astype(jnp.bfloat16)
                    out_ref[1, 0, i, pl.ds(start, tile), lane : lane + 128] = (
                        total[0] - total[1]
                    ).astype(jnp.bfloat16)
                    return c

                lax.fori_loop(0, first_rows, row, 0, unroll=8)
                return carry

            lax.fori_loop(0, width // tile, columns, 0)


def tiles(meta, pick, first_in, second_in, first_x, second_x, slots, win_dev, width):
    nwin, first_in_rows, bins = first_in.shape[1:]
    first_rows = first_in_rows // (2 * win_dev)
    whole = second_in.shape[1]
    shape = (2, slots, first_rows, width, bins)
    first_specs = [
        pl.BlockSpec((1, 1, first_in_rows, bins), lambda s, m, p: (p[s], m[2], 0, 0))
    ] + [
        pl.BlockSpec((1, 1, first_in_rows, bins), lambda s, m, p, k=k: (k, p[s], 0, 0))
        for k in range(nwin - 1)
    ]
    second_specs = [pl.BlockSpec((1, whole, bins), lambda s, m, p: (p[s], 0, 0))] + [
        pl.BlockSpec((1, 1, whole, bins), lambda s, m, p, k=k: (k, p[s], 0, 0))
        for k in range(nwin - 1)
    ]
    windows = nwin * win_dev
    return pl.pallas_call(
        functools.partial(
            tiles_kernel, nwin=nwin, win_dev=win_dev, first_rows=first_rows, width=width
        ),
        grid_spec=pltpu.PrefetchScalarGridSpec(
            num_scalar_prefetch=2,
            grid=(slots,),
            in_specs=first_specs + second_specs,
            out_specs=pl.BlockSpec(
                (2, 1, first_rows, width, bins), lambda s, m, p: (0, s, 0, 0, 0)
            ),
            scratch_shapes=[
                pltpu.VMEM((bins // 128, 3 * windows, first_rows, 128), jnp.float32),
                pltpu.VMEM((3 * windows, width, bins), jnp.float32),
            ],
        ),
        out_shape=jax.ShapeDtypeStruct(shape, jnp.bfloat16),
        compiler_params=pltpu.CompilerParams(vmem_limit_bytes=48 * MIB),
        cost_estimate=pl.CostEstimate(
            flops=16 * windows * math.prod(shape), bytes_accessed=12 * MIB, transcendentals=0
        ),
    )(meta, pick, first_in, *[first_x] * (nwin - 1), second_in, *[second_x] * (nwin - 1))


def shards(table, traces, block_members, pair_blocks, pair_owner):
    width = block_members.shape[1]
    local_rows, win_dev, samples = traces.shape
    owners = lax.axis_size("blk")
    nwin = lax.axis_size("win")
    slots = 2 * PAIR_DEV
    meta = jnp.stack([lax.axis_index(name) for name in ("blk", "frq", "win")]).astype(jnp.int32)
    spill, first_send, second_local, mask, pick = spectra(
        meta,
        pair_blocks.reshape(-1),
        pair_owner.reshape(-1),
        block_members,
        traces.reshape(local_rows * win_dev, samples),
        table,
        owners,
        nwin,
        win_dev,
        slots,
    )
    arrived = exchange(spill, first_send, second_local, mask)
    return tiles(meta, pick, *arrived, slots, win_dev, width)


def solution(mesh):
    placed = (
        P(("parts", "blk"), "win", None),
        P(("parts", "blk"), None),
        P("parts", None),
        P("parts", None),
    )

    def whole(traces, block_members, pair_blocks, pair_owner):
        table = jnp.asarray(dft_tables(traces.shape[2], mesh.shape["frq"]))
        return jax.shard_map(
            shards,
            mesh=mesh,
            in_specs=(P(None, None, None),) + placed,
            out_specs=P(None, ("parts", "blk"), "win", None, "frq"),
            check_vma=False,
        )(table, traces, block_members, pair_blocks, pair_owner)

    return whole
```

```python
import functools
import math

import jax
import jax.numpy as jnp
import numpy as np
from jax import lax
from jax.experimental import pallas as pl
from jax.experimental.pallas import tpu as pltpu
from jax.sharding import PartitionSpec as P

FREQS = 512
PAIR_DEV = 2

eps_time = 1e-05
eps_power = 1e-06
MIB = 1024 * 1024


def dft_tables(samples, parts):
    bins_dev = FREQS // parts
    t = np.arange(samples, dtype=np.int64)[:, None]
    k = np.arange(1, FREQS + 1, dtype=np.int64)[None, :]
    angles = (t * k % samples).astype(np.float32) * np.float32(2.0 * math.pi / samples)
    cos = np.cos(angles.astype(np.float64)).reshape(samples, parts, bins_dev)
    sin = np.sin(angles.astype(np.float64)).reshape(samples, parts, bins_dev)
    table = np.concatenate([cos, -sin], axis=2).transpose(1, 0, 2)
    return table.astype(np.float32).astype(jnp.bfloat16)


def spectra_kernel(
    meta_ref, blocks_ref, owner_ref, members_ref, x_ref, table_ref,
    spill, first_send, second_local, mask, pick, spectra, perm, *, row_tile, win_dev,
):
    step = pl.program_id(0)
    block_count, width = members_ref.shape
    owners, nwin, first_rows, bins = first_send.shape
    pairs_dev = spill.shape[0]
    slots = pick.shape[0] // 2
    x = x_ref[...].astype(jnp.float32)
    centre = x - jnp.mean(x, axis=1, keepdims=True)
    spread = jnp.mean(centre * centre, axis=1, keepdims=True)
    normal = (centre * lax.rsqrt(spread + eps_time)).astype(jnp.bfloat16)
    product = jnp.dot(normal, table_ref[0], preferred_element_type=jnp.float32)
    start = pl.multiple_of(step * row_tile, row_tile)
    spectra[pl.ds(start, row_tile), :] = product.astype(jnp.bfloat16)

    @pl.when(step == pl.num_programs(0) - 1)
    def _():
        me = meta_ref[0]
        rows = spectra.shape[0]
        chunk = win_dev * width
        half = width // nwin
        local = members_ref[...] % (rows // win_dev) * win_dev
        place = jnp.concatenate([local + w for w in range(win_dev)], axis=1)
        for block in range(block_count):
            row = lax.broadcasted_iota(jnp.int32, (rows, chunk), 0)
            onehot = jnp.where(row == place[block : block + 1, :], 1.0, 0.0).astype(jnp.bfloat16)
            perm[block] = lax.dot_general(
                onehot, spectra[...], (((0,), (0,)), ((), ())), preferred_element_type=jnp.float32
            ).astype(jnp.bfloat16)

        def whole_block(out, n, block):
            inside = (block >= 0) & (block < block_count)

            @pl.when(inside)
            def _():
                for part in range(2):
                    out[n, part * chunk : part * chunk + chunk, :] = perm[
                        block, :, part * bins : part * bins + bins
                    ]

            @pl.when(jnp.logical_not(inside))
            def _():
                out[n] = jnp.zeros(out.shape[1:], out.dtype)

        def halves(n, block):
            @pl.when(block >= 0)
            def _():
                for h in range(nwin):
                    for part in range(2):
                        for w in range(win_dev):
                            at = (part * win_dev + w) * half
                            first_send[n, h, at : at + half, :] = perm[
                                block,
                                w * width + h * half : w * width + h * half + half,
                                part * bins : part * bins + bins,
                            ]

            @pl.when(block < 0)
            def _():
                first_send[n] = jnp.zeros(first_send.shape[1:], first_send.dtype)

        before = jnp.maximum(me - 1, 0) * pairs_dev
        for q in range(pairs_dev):
            whole_block(spill, q, blocks_ref[before + q, 1] - me * block_count)

        def to_owner(o, carry):
            first, second = jnp.int32(-1), jnp.int32(-1)
            for q in range(pairs_dev):
                pair = me * pairs_dev + q
                hit = owner_ref[pair, 0] == o
                first_end = blocks_ref[pair, 0] - me * block_count
                second_end = blocks_ref[pair, 1] - me * block_count
                first = jnp.where(hit, first_end, first)
                second = jnp.where(hit, second_end, second)
                value = jnp.where(hit & (second_end >= block_count), 1.0, 0.0)
                mask[o, q : q + 1, :] = jnp.full((1, bins), value, jnp.float32)
            halves(o, first)
            whole_block(second_local, o, second)
            return carry

        lax.fori_loop(0, owners, to_owner, 0)

        for n in range(2 * slots):
            pick[n] = 0

        def from_group(g, rank):
            hit = owner_ref[g * pairs_dev, 0] == me
            for q in range(1, pairs_dev):
                hit = hit | (owner_ref[g * pairs_dev + q, 0] == me)

            @pl.when(hit & (rank < slots))
            def _():
                pick[rank] = g
                pick[slots + rank] = 1

            return rank + hit.astype(jnp.int32)

        lax.fori_loop(0, owners, from_group, jnp.int32(0))


def spectra(meta, pair_blocks, pair_owner, members, x, table, owners, nwin, win_dev, slots):
    rows, samples = x.shape
    cols = table.shape[2]
    bins = cols // 2
    block_count, width = members.shape
    chunk = win_dev * width
    row_tile = rows // 2
    whole = 2 * chunk
    shapes = [
        jax.ShapeDtypeStruct((PAIR_DEV, whole, bins), jnp.bfloat16),
        jax.ShapeDtypeStruct((owners, nwin, whole // nwin, bins), jnp.bfloat16),
        jax.ShapeDtypeStruct((owners, whole, bins), jnp.bfloat16),
        jax.ShapeDtypeStruct((owners, PAIR_DEV, bins), jnp.float32),
        jax.ShapeDtypeStruct((2 * slots,), jnp.int32),
    ]

    def fixed(shape):
        return pl.BlockSpec(shape, lambda i, *_: (0,) * len(shape))

    return pl.pallas_call(
        functools.partial(spectra_kernel, row_tile=row_tile, win_dev=win_dev),
        grid_spec=pltpu.PrefetchScalarGridSpec(
            num_scalar_prefetch=3,
            grid=(rows // row_tile,),
            in_specs=[
                fixed(members.shape),
                pl.BlockSpec((row_tile, samples), lambda i, *_: (i, 0)),
                pl.BlockSpec((1, samples, cols), lambda i, m, *_: (m[1], 0, 0)),
            ],
            out_specs=[fixed(s.shape) for s in shapes[:-1]]
            + [pl.BlockSpec(memory_space=pltpu.SMEM)],
            scratch_shapes=[
                pltpu.VMEM((rows, cols), jnp.bfloat16),
                pltpu.VMEM((block_count, chunk, cols), jnp.bfloat16),
            ],
        ),
        out_shape=shapes,
        compiler_params=pltpu.CompilerParams(vmem_limit_bytes=48 * MIB),
        cost_estimate=pl.CostEstimate(
            flops=2 * rows * samples * cols, bytes_accessed=8 * MIB, transcendentals=rows
        ),
    )(meta, pair_blocks, pair_owner, members, x, table)


def exchange_kernel(
    n, nwin, spill, first_send, second_local, mask,
    first_out, second_out, first_x, second_x,
    spill_in, second_send,
    spill_sems, zf_send, zf_recv, zs_send, zs_recv, xf_send, xf_recv, xs_send, xs_recv, own_sems,
):
    me = lax.axis_index("blk")
    my_win = lax.axis_index("win")
    pairs_dev = spill.shape[0]

    def along(d):
        return {"blk": lax.rem(me + d, n)}

    def across(shift):
        return {"win": lax.rem(my_win + shift, nwin)}

    def remote(src, dst, send, recv, device):
        return pltpu.make_async_remote_copy(
            src_ref=src, dst_ref=dst, send_sem=send, recv_sem=recv,
            device_id=device, device_id_type=pl.DeviceIdType.MESH,
        )

    barrier = pltpu.get_barrier_semaphore()
    for d in range(1, n):
        pl.semaphore_signal(barrier, inc=1, device_id=along(d), device_id_type=pl.DeviceIdType.MESH)
    for s in range(1, nwin):
        pl.semaphore_signal(barrier, inc=1, device_id=across(s), device_id_type=pl.DeviceIdType.MESH)
    pl.semaphore_wait(barrier, n + nwin - 2)

    to_left = remote(spill, spill_in, spill_sems.at[0], spill_sems.at[1], along(n - 1))

    @pl.when(me > 0)
    def _():
        to_left.start()

    def first_to(d):
        return remote(
            first_send.at[lax.rem(me + d, n)], first_out.at[me], zf_send.at[d], zf_recv.at[d], along(d)
        )

    def second_to(d):
        return remote(
            second_send.at[lax.rem(me + d, n)], second_out.at[me], zs_send.at[d], zs_recv.at[d], along(d)
        )

    def first_across(d, shift):
        source = lax.rem(me + n - d, n)
        other = lax.rem(my_win + shift, nwin)
        ref = first_send if d == 0 else first_out
        k = d * nwin + shift
        return remote(
            ref.at[source, other], first_x.at[shift - 1, source], xf_send.at[k], xf_recv.at[k], across(shift)
        )

    def second_across(d, shift):
        source = lax.rem(me + n - d, n)
        ref = second_send if d == 0 else second_out
        k = d * nwin + shift
        return remote(
            ref.at[source], second_x.at[shift - 1, source], xs_send.at[k], xs_recv.at[k], across(shift)
        )

    order = sorted(range(1, n), key=lambda d: min(d, n - d))
    for d in order:
        first_to(d).start()
    own_first = pltpu.make_async_copy(first_send.at[me], first_out.at[me], own_sems.at[0])
    own_first.start()
    for shift in range(1, nwin):
        first_across(0, shift).start()

    @pl.when(me == n - 1)
    def _():
        spill_in[...] = jnp.zeros_like(spill_in)

    @pl.when(me < n - 1)
    def _():
        to_left.wait_recv()

    for d in order + [0]:
        o = lax.rem(me + d, n)
        total = second_local[o].astype(jnp.float32)
        for q in range(pairs_dev):
            total = total + spill_in[q].astype(jnp.float32) * mask[o, q : q + 1, :]
        second_send[o] = total.astype(jnp.bfloat16)
        if d:
            second_to(d).start()
    own_second = pltpu.make_async_copy(second_send.at[me], second_out.at[me], own_sems.at[1])
    own_second.start()
    for shift in range(1, nwin):
        second_across(0, shift).start()

    for d in order:
        first_to(d).wait_recv()
        for shift in range(1, nwin):
            first_across(d, shift).start()
    for d in order:
        second_to(d).wait_recv()
        for shift in range(1, nwin):
            second_across(d, shift).start()
    own_first.wait()
    own_second.wait()

    @pl.when(me > 0)
    def _():
        to_left.wait_send()

    for d in order:
        first_to(d).wait_send()
        second_to(d).wait_send()
    for d in range(n):
        for shift in range(1, nwin):
            first_across(d, shift).wait()
            second_across(d, shift).wait()


def exchange(spill, first_send, second_local, mask):
    n, nwin, first_rows, bins = first_send.shape
    rows = second_local.shape[1]
    hbm = pl.BlockSpec(memory_space=pl.ANY)
    vmem = pl.BlockSpec(memory_space=pltpu.VMEM)
    dma = pltpu.SemaphoreType.DMA
    sent = jax.ShapeDtypeStruct
    return pl.pallas_call(
        functools.partial(exchange_kernel, n, nwin),
        in_specs=[hbm, hbm, vmem, vmem],
        out_specs=[hbm] * 4,
        out_shape=[
            sent(first_send.shape, jnp.bfloat16),
            sent(second_local.shape, jnp.bfloat16),
            sent((nwin - 1, n, first_rows, bins), jnp.bfloat16),
            sent((nwin - 1, n, rows, bins), jnp.bfloat16),
        ],
        scratch_shapes=[
            pltpu.VMEM(spill.shape, jnp.bfloat16),
            pltpu.VMEM(second_local.shape, jnp.bfloat16),
            dma((2,)),
            dma((n,)), dma((n,)), dma((n,)), dma((n,)),
            dma((n * nwin,)), dma((n * nwin,)), dma((n * nwin,)), dma((n * nwin,)),
            dma((2,)),
        ],
        compiler_params=pltpu.CompilerParams(
            collective_id=0, has_side_effects=True, vmem_limit_bytes=32 * MIB
        ),
        cost_estimate=pl.CostEstimate(flops=0, bytes_accessed=4 * MIB, transcendentals=0),
    )(spill, first_send, second_local, mask)


def tiles_kernel(meta_ref, pick_ref, *refs, nwin, win_dev, first_rows, width):
    firsts, seconds = refs[:nwin], refs[nwin : 2 * nwin]
    out_ref, left, right = refs[2 * nwin :]
    slots = pl.num_programs(0)
    slot = pl.program_id(0)
    windows = nwin * win_dev
    bins = out_ref.shape[4]
    filled = pick_ref[slots + slot]

    @pl.when(filled == 0)
    def _():
        out_ref[...] = jnp.zeros_like(out_ref)

    @pl.when(filled != 0)
    def _():
        def whitened(ends, rows, scale):
            real, imag = [], []
            for ref in ends:
                view = ref[...].reshape(2, win_dev, rows, bins).astype(jnp.float32)
                for w in range(win_dev):
                    real.append(view[0, w])
                    imag.append(view[1, w])
            power = sum(r * r + i * i for r, i in zip(real, imag)) * (1.0 / windows)
            gain = lax.rsqrt(power + eps_power) * scale
            return [r * gain for r in real], [i * gain for i in imag]

        real, imag = whitened(firsts, first_rows, 1.0 / windows)
        for w in range(windows):
            for term, value in enumerate((real[w] + imag[w], real[w], imag[w])):
                for part in range(bins // 128):
                    left[part, term * windows + w] = value[:, part * 128 : part * 128 + 128]
        real, imag = whitened(seconds, width, 1.0)
        for w in range(windows):
            right[w] = real[w]
            right[windows + w] = real[w] + imag[w]
            right[2 * windows + w] = real[w] - imag[w]

        tile = 16
        for lane in range(0, bins, 128):

            def columns(t, carry, lane=lane):
                start = pl.multiple_of(t * tile, tile)
                held = [
                    right[n, pl.ds(start, tile), lane : lane + 128] for n in range(3 * windows)
                ]

                def row(i, c):
                    total = []
                    for term in range(3):
                        acc = None
                        for w in range(windows):
                            n = term * windows + w
                            one = left[lane // 128, n, pl.ds(i, 1), :]
                            prod = jnp.broadcast_to(one, (tile, 128)) * held[n]
                            acc = prod if acc is None else acc + prod
                        total.append(acc)
                    out_ref[0, 0, i, pl.ds(start, tile), lane : lane + 128] = (
                        total[0] - total[2]
                    ).astype(jnp.bfloat16)
                    out_ref[1, 0, i, pl.ds(start, tile), lane : lane + 128] = (
                        total[0] - total[1]
                    ).astype(jnp.bfloat16)
                    return c

                lax.fori_loop(0, first_rows, row, 0, unroll=8)
                return carry

            lax.fori_loop(0, width // tile, columns, 0)


def tiles(meta, pick, first_in, second_in, first_x, second_x, slots, win_dev, width):
    nwin, first_in_rows, bins = first_in.shape[1:]
    first_rows = first_in_rows // (2 * win_dev)
    whole = second_in.shape[1]
    shape = (2, slots, first_rows, width, bins)
    first_specs = [
        pl.BlockSpec((1, 1, first_in_rows, bins), lambda s, m, p: (p[s], m[2], 0, 0))
    ] + [
        pl.BlockSpec((1, 1, first_in_rows, bins), lambda s, m, p, k=k: (k, p[s], 0, 0))
        for k in range(nwin - 1)
    ]
    second_specs = [pl.BlockSpec((1, whole, bins), lambda s, m, p: (p[s], 0, 0))] + [
        pl.BlockSpec((1, 1, whole, bins), lambda s, m, p, k=k: (k, p[s], 0, 0))
        for k in range(nwin - 1)
    ]
    windows = nwin * win_dev
    return pl.pallas_call(
        functools.partial(
            tiles_kernel, nwin=nwin, win_dev=win_dev, first_rows=first_rows, width=width
        ),
        grid_spec=pltpu.PrefetchScalarGridSpec(
            num_scalar_prefetch=2,
            grid=(slots,),
            in_specs=first_specs + second_specs,
            out_specs=pl.BlockSpec(
                (2, 1, first_rows, width, bins), lambda s, m, p: (0, s, 0, 0, 0)
            ),
            scratch_shapes=[
                pltpu.VMEM((bins // 128, 3 * windows, first_rows, 128), jnp.float32),
                pltpu.VMEM((3 * windows, width, bins), jnp.float32),
            ],
        ),
        out_shape=jax.ShapeDtypeStruct(shape, jnp.bfloat16),
        compiler_params=pltpu.CompilerParams(vmem_limit_bytes=48 * MIB),
        cost_estimate=pl.CostEstimate(
            flops=16 * windows * math.prod(shape), bytes_accessed=12 * MIB, transcendentals=0
        ),
    )(meta, pick, first_in, *[first_x] * (nwin - 1), second_in, *[second_x] * (nwin - 1))


def shards(table, traces, block_members, pair_blocks, pair_owner):
    width = block_members.shape[1]
    local_rows, win_dev, samples = traces.shape
    owners = lax.axis_size("blk")
    nwin = lax.axis_size("win")
    slots = 2 * PAIR_DEV
    meta = jnp.stack([lax.axis_index(name) for name in ("blk", "frq", "win")]).astype(jnp.int32)
    spill, first_send, second_local, mask, pick = spectra(
        meta,
        pair_blocks,
        pair_owner,
        block_members,
        traces.reshape(local_rows * win_dev, samples),
        table,
        owners,
        nwin,
        win_dev,
        slots,
    )
    arrived = exchange(spill, first_send, second_local, mask)
    return tiles(meta, pick, *arrived, slots, win_dev, width)


def solution(mesh):
    placed = (
        P(("parts", "blk"), "win", None),
        P(("parts", "blk"), None),
        P("parts", None),
        P("parts", None),
    )

    def whole(traces, block_members, pair_blocks, pair_owner):
        table = jnp.asarray(dft_tables(traces.shape[2], mesh.shape["frq"]))
        return jax.shard_map(
            shards,
            mesh=mesh,
            in_specs=(P(None, None, None),) + placed,
            out_specs=P(None, ("parts", "blk"), "win", None, "frq"),
            check_vma=False,
        )(table, traces, block_members, pair_blocks, pair_owner)

    return whole
```
